128 devices in a mesh: ctx: 32 (over x_lo, z, y), head: 4 (over x_hi, core).
Axes of the slice: x: 4 (x_hi: 2, x_lo: 2; x = x_hi * 2 + x_lo), y: 4, z: 4, core: 2. Of those that a mesh axis runs over, the one named last changes fastest.
Arguments:
- stretch_queries: bfloat16 [512, 128, 576], P('ctx', 'head'), may hold values from -500 to 500
- cache_latent: bfloat16 [8192, 576], P('ctx'), may hold values from -6 to 6
- doc_lengths: int32 [32], replicated, may hold values from 1 to 256, 6144 in all
- decode_queries: bfloat16 [128, 64, 576], P('ctx', 'head'), may hold values from -500 to 500
- w_attn_out: bfloat16 [64, 512, 7168], P('head', None, 'ctx'), may hold values from -0.25 to 0.25
- decode_hidden: bfloat16 [128, 7168], P('ctx'), may hold values from -6 to 6
- norm_gain: float32 [7168], replicated, may hold values from 0.1 to 1.9
- w_gate: bfloat16 [32, 7168, 2048], P('ctx', None, 'head'), may hold values from -0.0625 to 0.0625
- w_up: bfloat16 [32, 7168, 2048], P('ctx', None, 'head'), may hold values from -0.0625 to 0.0625
- w_down: bfloat16 [32, 2048, 7168], P('ctx', 'head'), may hold values from -0.125 to 0.125
- routes: int32 [3, 128, 8], P(None, 'ctx'), may hold values from 0 to 31, all different within a row; in each aligned block of 4 rows (0 to 3, 4 to 7, ..., all dimensions but the last counted through in order) at most 2 rows name the same one
- gate_weights: float32 [3, 128, 8], P(None, 'ctx'), may hold values from 0.05 to 0.4
Outputs:
- stretch_latent: bfloat16 [512, 128, 512], P('ctx', 'head')
- decode_out: bfloat16 [128, 7168], P('ctx')
The draws below stay inside these ranges and needn't reach their ends.
Inputs may be any that keep to these rules, and one draw needn't show every extreme that they name: `routes`: in each step, among the 4 rows of one device, no expert is named by more than 2 rows, a bound that some block reaches; a row names 8 different experts. `doc_lengths`: every block has at least one used position and some block is full.
All inputs are finite; a program needn't handle non-finite values.
Results may differ from the reference program's by a relative error of at most 0.023.
Values may be sent and summed in bfloat16 or wider, within the bound.
No kernel may reach another device: no remote copies, remote signals or barrier semaphores. Data moves between devices by JAX's collectives and lax.ppermute only.
A program may use at most 128 MiB of HBM per device.

```python
import math
import jax
import jax.numpy as jnp
import numpy as np
from jax import lax

D = 7168
HEADS = 128
KV_RANK = 512
ROPE = 64
FF = 2048
TOPK = 8
CACHE_DEV = 256
ROW_DEV = 4
STEPS = 3
DEC_HEADS = 64
STRETCH = 512
CTX_LEN = 8192
DOCS = 32
ROWS = 128
EXPERTS = 32
CAP = 2
N_CTX = 32


def draw_stretch_queries(key, part):
    key = jax.random.fold_in(key, 11)
    values = jnp.clip(jax.random.normal(key, (STRETCH, HEADS, KV_RANK + ROPE), jnp.float32), -5.0, 5.0)
    return values.astype(jnp.bfloat16)


def draw_decode_queries(key, part):
    key = jax.random.fold_in(key, 13)
    values = jnp.clip(jax.random.normal(key, (ROWS, DEC_HEADS, KV_RANK + ROPE), jnp.float32), -5.0, 5.0)
    return values.astype(jnp.bfloat16)


def block_scale(rng, dims, shards, smallest, high):
    level = 1.0
    for position, shards_of in shards:
        heights = jax.random.uniform(jax.random.fold_in(jax.random.fold_in(rng, 6), position), (shards_of,), jnp.float32, smallest / len(shards), high / len(shards))
        level = level * jnp.repeat(jnp.exp(heights), dims[position] // shards_of).reshape((-1,) + (1,) * (len(dims) - 1 - position))
    return level


def profile(count, total, limit, slope):
    loads = [(1 << 20) // math.isqrt(standing ** slope) + 1 for standing in range(2, count + 1)]
    spare, counts = total - limit - (count - 1), [1] * (count - 1)
    while spare > 0:
        movable = [i for i in range(count - 1) if counts[i] < limit]
        pool, remaining = sum([loads[i] for i in movable]), spare
        for i in movable:
            extra = min(limit - counts[i], max(1, remaining * loads[i] // pool), spare)
            counts[i] = counts[i] + extra
            spare = spare - extra
    return np.array([limit] + counts)


def ragged(key, count, total, limit, lean):
    if count == 2:
        one = jax.random.randint(key, (), max(1, total - limit), min(limit, total - 1) + 1)
        return jnp.stack([one, total - one])
    tallies = jnp.asarray(profile(count, total, limit, lean), jnp.int32)
    couples = (count - 1) // 2
    source_of, sink = tallies[1:1 + 2 * couples:2], tallies[2:2 + 2 * couples:2]
    room = jnp.minimum(source_of - 1, limit - sink)
    passed = jax.random.randint(jax.random.fold_in(key, 1), (couples,), 0, 1 << 20) % (room + 1)
    tallies = tallies.at[1:1 + 2 * couples:2].set(source_of - passed).at[2:2 + 2 * couples:2].set(sink + passed)
    return tallies[jax.random.permutation(jax.random.fold_in(key, 2), count)]


def deal_out(own_key, own, number, rows, count, top, most, lean):
    ranking = jax.random.permutation(own_key, count)
    crowded, ordinary = portions_of(count, rows * top, most, lean, True), portions_of(count, rows * top, most, lean, False)
    places = jnp.arange(count)

    def named(lengths, offset_by):
        used = int((lengths > 0).sum())
        fixed = max(1, used // 4)
        moved = fixed + (places - fixed + offset_by * (used - fixed)) % max(1, count - fixed)
        return jnp.zeros((count,), jnp.int32).at[ranking[jnp.where(places < fixed, places, moved)]].set(jnp.asarray(lengths, jnp.int32))

    lengths = jnp.where(number % 4 == 0, named(crowded, number // 4), named(ordinary, number - number // 4 - 1))
    mixed = jax.random.permutation(jax.random.fold_in(own, 3), count)
    source_of, sink = mixed[0:count // 2 * 2:2], mixed[1:count // 2 * 2:2]
    slack = jnp.minimum(lengths[source_of] - 1, most - lengths[sink]) // 2
    slack = jnp.where((source_of == ranking[0]) | (sink == ranking[0]) | (lengths[sink] == 0), 0, jnp.maximum(slack, 0))
    moved = jax.random.randint(jax.random.fold_in(own, 4), (count // 2,), 0, 1 << 20) % (slack + 1)
    lengths = lengths.at[source_of].add(-moved).at[sink].add(moved)
    items = jnp.searchsorted(jnp.cumsum(lengths), jnp.arange(rows * top), side="right").astype(jnp.int32)
    grid = items.reshape(top, rows).T
    grid = grid[jax.random.permutation(jax.random.fold_in(own, 1), rows)]
    offset_by = jax.random.randint(jax.random.fold_in(own, 2), (rows, 1), 0, top)
    return jnp.take_along_axis(grid, (jnp.arange(top)[None, :] + offset_by) % top, axis=1)


def portions_of(count, total, reach, slope, full):
    loads = [(1 << 20) // math.isqrt(grade ** slope) + 1 for grade in range(1, count + 1)]
    largest = reach if full else min(reach, max(-(-total // count), total * loads[0] // sum(loads)))
    least = 1 if total - largest >= count - 1 else 0
    counts, spare = [largest] + [least] * (count - 1), total - largest - least * (count - 1)
    while spare > 0:
        free = [i for i in range(1, count) if counts[i] < largest] or [i for i in range(1, count) if counts[i] < reach]
        pool, budget = sum([loads[i] for i in free]), spare
        for i in free:
            addition = min(reach - counts[i], max(1, budget * loads[i] // pool), spare)
            counts[i] = counts[i] + addition
            spare = spare - addition
    return np.array(counts)


def noise(stream_key, dims, deviation, reach, shards=(), kind=jnp.bfloat16):
    factor_of = block_scale(stream_key, dims, shards, -0.22, 0.18) if shards else 1.0
    values = jax.random.normal(stream_key, dims, jnp.float32) * deviation * factor_of
    return jnp.minimum(jnp.maximum(values, -reach), reach).astype(kind)


def setup_inputs(seed: int = 0) -> dict:
    arg_keys = jax.random.split(jax.random.key(seed), 13)
    stretch_queries = draw_stretch_queries(jax.random.fold_in(arg_keys[12], 71), 0)
    cache_latent = noise(arg_keys[1], (CTX_LEN, KV_RANK + ROPE), 1.0, 6.0, ((0, 32),))
    doc_lengths = ragged(arg_keys[2], DOCS, CTX_LEN * 3 // 4, CACHE_DEV, 1).astype(jnp.int32)
    decode_queries = draw_decode_queries(jax.random.fold_in(arg_keys[12], 71), 0)
    w_attn_out = noise(arg_keys[4], (DEC_HEADS, KV_RANK, D), KV_RANK ** -0.5, 0.25, ((0, 4), (2, 32)))
    decode_hidden = noise(arg_keys[5], (ROWS, D), 1.0, 6.0, ((0, 32),))
    norm_gain = jnp.clip(1.0 + 0.18 * jax.random.normal(arg_keys[6], (D,), jnp.float32), 0.1, 1.9)
    w_gate = noise(arg_keys[7], (EXPERTS, D, FF), D ** -0.5, 0.0625, ((0, 32), (2, 4)))
    w_up = noise(arg_keys[8], (EXPERTS, D, FF), D ** -0.5, 0.0625, ((0, 32), (2, 4)))
    w_down = noise(arg_keys[9], (EXPERTS, FF, D), FF ** -0.5, 0.125, ((0, 32), (1, 4)))
    routes_keys = jax.random.split(jax.random.fold_in(arg_keys[10], 1), STEPS * ROWS // ROW_DEV)
    routes_turns = jax.random.permutation(jax.random.fold_in(arg_keys[10], 3), STEPS * ROWS // ROW_DEV)
    routes = jax.vmap(lambda own, number: deal_out(jax.random.fold_in(arg_keys[10], 2), own, number, ROW_DEV, EXPERTS, TOPK, CAP, 1))(routes_keys, routes_turns).reshape((STEPS, ROWS, TOPK))
    gate_weights = jnp.clip(0.05 + 0.35 * jax.random.uniform(arg_keys[11], (STEPS, ROWS, TOPK), jnp.float32) ** block_scale(arg_keys[11], (STEPS, ROWS, TOPK), ((1, 32),), -0.2, 0.2), 0.05, 0.4)
    return {"stretch_queries": stretch_queries, "cache_latent": cache_latent, "doc_lengths": doc_lengths, "decode_queries": decode_queries, "w_attn_out": w_attn_out, "decode_hidden": decode_hidden, "norm_gain": norm_gain, "w_gate": w_gate, "w_up": w_up, "w_down": w_down, "routes": routes, "gate_weights": gate_weights}


score_scale = 0.07216878364870322

def usable_mask(doc_lengths):
    place = jnp.arange(CTX_LEN, dtype=jnp.int32)
    owner = (place // CACHE_DEV).astype(jnp.int32)
    return place % CACHE_DEV < doc_lengths[owner]

def attend_heads(query_block, cache_latent, usable):
    latent_part = cache_latent[:, :KV_RANK]

    def one_head(queries):
        scores = jnp.dot(queries, cache_latent.T, preferred_element_type=jnp.float32) * score_scale
        scores = jnp.where(usable[None, :], scores, -1e+30)
        top_score = lax.optimization_barrier(jnp.max(scores, axis=1, keepdims=True))
        probs = jnp.where(usable[None, :], jnp.exp(scores - top_score), 0.0)
        total = lax.optimization_barrier(jnp.sum(probs, axis=1, keepdims=True))
        mixed = jnp.dot(probs.astype(jnp.bfloat16), latent_part, preferred_element_type=jnp.float32)
        return (mixed / total).astype(jnp.bfloat16)
    by_head = lax.map(one_head, jnp.swapaxes(query_block, 0, 1))
    return jnp.swapaxes(by_head, 0, 1)

def reference(stretch_queries, cache_latent, doc_lengths, decode_queries, w_attn_out, decode_hidden, norm_gain, w_gate, w_up, w_down, routes, gate_weights):
    usable = usable_mask(doc_lengths)
    stretch_latent = attend_heads(stretch_queries, cache_latent, usable)
    dec_latent = attend_heads(decode_queries, cache_latent, usable)

    def head_term(carry, inputs):
        latent_rows, weight = inputs
        return (carry + jnp.dot(latent_rows, weight, preferred_element_type=jnp.float32), None)
    attn_sum, _ = lax.scan(head_term, jnp.zeros((ROWS, D), jnp.float32), (jnp.swapaxes(dec_latent, 0, 1), w_attn_out))
    attn_out = attn_sum.astype(jnp.bfloat16)
    state = (decode_hidden.astype(jnp.float32) + attn_out.astype(jnp.float32)).astype(jnp.bfloat16)
    slots_most = N_CTX * CAP
    for step in range(STEPS):
        state_f = state.astype(jnp.float32)
        normed = (state_f * lax.rsqrt(lax.optimization_barrier(jnp.mean(state_f * state_f, axis=1, keepdims=True)) + 1e-06) * norm_gain).astype(jnp.bfloat16)
        chosen = routes[step]
        weights = gate_weights[step]

        def per_expert(carry, inputs):
            gate_w, up_w, down_w, expert = inputs
            weight_row = lax.optimization_barrier(jnp.sum(jnp.where(chosen == expert, weights, 0.0), axis=1))
            used = jnp.any(chosen == expert, axis=1).astype(jnp.int32)
            order = jnp.argsort(1 - used, stable=True)[:slots_most].astype(jnp.int32)
            picked = normed[order]
            gate = jnp.dot(picked, gate_w, preferred_element_type=jnp.float32)
            upper = jnp.dot(picked, up_w, preferred_element_type=jnp.float32)
            inner = (jax.nn.silu(gate) * upper).astype(jnp.bfloat16)
            result = jnp.dot(inner, down_w, preferred_element_type=jnp.float32).astype(jnp.bfloat16)
            term = weight_row[order][:, None] * result.astype(jnp.float32)
            return (carry.at[order].add(term), None)
        added, _ = lax.scan(per_expert, jnp.zeros((ROWS, D), jnp.float32), (w_gate, w_up, w_down, jnp.arange(EXPERTS, dtype=jnp.int32)))
        state = (state_f + added).astype(jnp.bfloat16)
    return (stretch_latent, state)
```

```python
import functools

import jax
import jax.numpy as jnp
from jax import lax
from jax.experimental import pallas as pl
from jax.experimental.pallas import tpu as pltpu
from jax.sharding import Mesh, PartitionSpec as P

KV_RANK = 512
STEPS = 3
SLOTS = 2
SCALE = 0.07216878364870322
MASKED = -1e30

SPLIT = {"ctx": (("x_lo", 2), ("z", 4), ("y", 4)), "head": (("x_hi", 2), ("core", 2))}
CTX = ("x_lo", "z", "y")
HEAD = ("x_hi", "core")
SHARDS = ("x_lo", "z")
LANE = CTX + ("x_hi",)


def shift(x, axis, by):
    n = lax.axis_size(axis)
    return lax.ppermute(x, axis, [(i, (i + by) % n) for i in range(n)])


def spread(x, axes):
    n = lax.axis_size(axes)
    return lax.all_to_all(jnp.broadcast_to(x[None], (n,) + x.shape), axes, 0, 0, tiled=True)


def dot_t(a, b):
    return lax.dot_general(a, b, (((1,), (1,)), ((), ())), preferred_element_type=jnp.float32)


def dec_attn_kernel(q_ref, kv_ref, bias_ref, out_ref):
    kv = kv_ref[...]
    s = dot_t(q_ref[...], kv) * SCALE + bias_ref[...]
    top = jnp.max(s, axis=1, keepdims=True)
    p = jnp.exp(s - top)
    total = jnp.sum(p, axis=1, keepdims=True)
    acc = jnp.dot(p.astype(jnp.bfloat16), kv[:, :KV_RANK], preferred_element_type=jnp.float32)
    out_ref[:, :KV_RANK] = (acc / total).astype(jnp.bfloat16)
    lse = jnp.broadcast_to(top + jnp.log(total), (q_ref.shape[0], 128))
    hi = lse.astype(jnp.bfloat16).astype(jnp.float32)
    mid = (lse - hi).astype(jnp.bfloat16).astype(jnp.float32)
    low = lse - hi - mid
    lane = lax.broadcasted_iota(jnp.int32, lse.shape, 1)
    out_ref[:, KV_RANK:] = jnp.where(
        lane == 0, hi, jnp.where(lane == 1, mid, jnp.where(lane == 2, low, 0.0))
    ).astype(jnp.bfloat16)


def combine_kernel(parts_ref, out_ref):
    n = parts_ref.shape[0]
    lses = [
        jnp.sum(parts_ref[i, :, KV_RANK:].astype(jnp.float32), axis=1, keepdims=True)
        for i in range(n)
    ]
    top = functools.reduce(jnp.maximum, lses)
    shares = [jnp.exp(x - top) for x in lses]
    total = functools.reduce(jnp.add, shares)
    acc = sum(shares[i] * parts_ref[i, :, :KV_RANK].astype(jnp.float32) for i in range(n))
    out_ref[...] = (acc / total).astype(jnp.bfloat16)


def prefill_kernel(q_ref, kv_a, kv_b, bias_a, bias_b, out_ref, top_ref, total_ref, acc_ref):
    step = pl.program_id(0)

    @pl.when(step == 0)
    def _():
        top_ref[...] = jnp.full_like(top_ref, MASKED)
        total_ref[...] = jnp.zeros_like(total_ref)
        acc_ref[...] = jnp.zeros_like(acc_ref)

    q = q_ref[...]
    for kv_ref, bias_ref in ((kv_a, bias_a), (kv_b, bias_b)):
        kv = kv_ref[...]
        s = dot_t(q, kv) * SCALE + bias_ref[...]
        old = top_ref[...]
        top = jnp.maximum(old, jnp.max(s, axis=1, keepdims=True))
        p = jnp.exp(s - top)
        fade = jnp.exp(old - top)
        total_ref[...] = total_ref[...] * fade + jnp.sum(p, axis=1, keepdims=True)
        acc_ref[...] = acc_ref[...] * fade + jnp.dot(
            p.astype(jnp.bfloat16), kv[:, :KV_RANK], preferred_element_type=jnp.float32
        )
        top_ref[...] = top

    @pl.when(step == pl.num_programs(0) - 1)
    def _():
        out_ref[...] = (acc_ref[...] / total_ref[...]).astype(jnp.bfloat16)


def prefill(q, kv_a, kv_b, bias_a, bias_b):
    rows, width = q.shape
    count = kv_a.shape[0]
    block = 1024
    kv_spec = pl.BlockSpec((block, width), lambda i: (i, 0))
    bias_spec = pl.BlockSpec((1, block), lambda i: (0, i))
    return pl.pallas_call(
        prefill_kernel,
        grid=(count // block,),
        in_specs=[pl.BlockSpec((rows, width), lambda i: (0, 0)), kv_spec, kv_spec, bias_spec, bias_spec],
        out_specs=pl.BlockSpec((rows, KV_RANK), lambda i: (0, 0)),
        out_shape=jax.ShapeDtypeStruct((rows, KV_RANK), jnp.bfloat16),
        scratch_shapes=[
            pltpu.VMEM((rows, 1), jnp.float32),
            pltpu.VMEM((rows, 1), jnp.float32),
            pltpu.VMEM((rows, KV_RANK), jnp.float32),
        ],
        compiler_params=pltpu.CompilerParams(vmem_limit_bytes=40 << 20),
        cost_estimate=pl.CostEstimate(
            flops=2 * rows * 2 * count * (width + KV_RANK),
            bytes_accessed=4 * count * width,
            transcendentals=2 * rows * count,
        ),
        name="prefill",
    )(q, kv_a, kv_b, bias_a, bias_b)


def inner_kernel(x_ref, gain_ref, gate_ref, up_ref, out_ref, x_scr, gate_acc, up_acc):
    step = pl.program_id(0)
    chunk = gate_ref.shape[0]

    @pl.when(step == 0)
    def _():
        halves = x_ref.shape[0]
        width = x_ref.shape[2]
        xs = [x_ref[i].astype(jnp.float32) for i in range(halves)]
        square = sum(jnp.sum(x * x, axis=1, keepdims=True) for x in xs) / (halves * width)
        scale = lax.rsqrt(square + 1e-06)
        for i in range(halves):
            x = (xs[i] * scale * gain_ref[:, i * width : (i + 1) * width]).astype(jnp.bfloat16)
            for j in range(width // chunk):
                x_scr[i * (width // chunk) + j] = x[:, j * chunk : (j + 1) * chunk]
        gate_acc[...] = jnp.zeros_like(gate_acc)
        up_acc[...] = jnp.zeros_like(up_acc)

    x = x_scr[step]
    gate_acc[...] += jnp.dot(x, gate_ref[...], preferred_element_type=jnp.float32)
    up_acc[...] += jnp.dot(x, up_ref[...], preferred_element_type=jnp.float32)

    @pl.when(step == pl.num_programs(0) - 1)
    def _():
        out_ref[...] = (jax.nn.silu(gate_acc[...]) * up_acc[...]).astype(jnp.bfloat16)


def expert_inner(x, gain, w_gate, w_up):
    halves, rows, width = x.shape
    depth, hidden = w_gate.shape
    chunk = 896
    w_spec = pl.BlockSpec((chunk, hidden), lambda i: (i, 0))
    return pl.pallas_call(
        inner_kernel,
        grid=(depth // chunk,),
        in_specs=[
            pl.BlockSpec(x.shape, lambda i: (0, 0, 0)),
            pl.BlockSpec((1, depth), lambda i: (0, 0)),
            w_spec,
            w_spec,
        ],
        out_specs=pl.BlockSpec((rows, hidden), lambda i: (0, 0)),
        out_shape=jax.ShapeDtypeStruct((rows, hidden), jnp.bfloat16),
        scratch_shapes=[
            pltpu.VMEM((depth // chunk, rows, chunk), jnp.bfloat16),
            pltpu.VMEM((rows, hidden), jnp.float32),
            pltpu.VMEM((rows, hidden), jnp.float32),
        ],
        compiler_params=pltpu.CompilerParams(vmem_limit_bytes=24 << 20),
        cost_estimate=pl.CostEstimate(
            flops=4 * rows * depth * hidden, bytes_accessed=4 * depth * hidden, transcendentals=rows * hidden
        ),
        name="expert_inner",
    )(x, gain, w_gate, w_up)


def down_kernel(core_ref, inner_ref, own_ref, other_ref, out_ref):
    core = core_ref[0]
    out_ref[...] = (
        jnp.dot(inner_ref[core], own_ref[...], preferred_element_type=jnp.float32)
        + jnp.dot(inner_ref[1 - core], other_ref[...], preferred_element_type=jnp.float32)
    ).astype(jnp.bfloat16)


def expert_down(core, inner, w_down, w_other):
    cores, rows, hidden = inner.shape
    width = w_other.shape[1]
    block = 896
    steps = width // block
    return pl.pallas_call(
        down_kernel,
        grid_spec=pltpu.PrefetchScalarGridSpec(
            num_scalar_prefetch=1,
            grid=(steps,),
            in_specs=[
                pl.BlockSpec(inner.shape, lambda i, core: (0, 0, 0)),
                pl.BlockSpec((hidden, block), lambda i, core: (0, core[0] * steps + i)),
                pl.BlockSpec((hidden, block), lambda i, core: (0, i)),
            ],
            out_specs=pl.BlockSpec((rows, block), lambda i, core: (0, i)),
        ),
        out_shape=jax.ShapeDtypeStruct((rows, width), jnp.bfloat16),
        compiler_params=pltpu.CompilerParams(vmem_limit_bytes=24 << 20),
        cost_estimate=pl.CostEstimate(
            flops=4 * rows * hidden * width, bytes_accessed=4 * hidden * width, transcendentals=0
        ),
        name="expert_down",
    )(core, inner, w_down, w_other)


def per_device(
    stretch_queries,
    cache_latent,
    doc_lengths,
    decode_queries,
    w_attn_out,
    decode_hidden,
    norm_gain,
    w_gate,
    w_up,
    w_down,
    routes,
    gate_weights,
):
    tokens, heads, width = stretch_queries.shape
    rows, dec_heads, _ = decode_queries.shape
    block = cache_latent.shape[0]
    half = block // 2
    ctx_size = lax.axis_size(CTX)
    model = decode_hidden.shape[1]
    core = lax.axis_index("core")
    x_hi = lax.axis_index("x_hi")
    quarter = model // 4
    my_quarter = core * 2 + x_hi

    mine = lax.dynamic_slice_in_dim(cache_latent, core * half, half, 0)

    line = jnp.stack([mine] + [shift(mine, "y", by) for by in (1, 3, 2)])
    dec_q = decode_queries.reshape(rows * dec_heads, width)
    group_q = spread(dec_q, SHARDS)
    shards = group_q.shape[0]
    line_kv = lax.all_gather(line, "core", axis=0)
    y = lax.axis_index("y")
    line_at = lax.axis_index(SHARDS) * 4 + (y - jnp.array([0, 1, 3, 2], jnp.int32)) % 4
    place = jnp.arange(block, dtype=jnp.int32).reshape(2, 1, half)
    line_bias = jnp.where(place < doc_lengths[line_at][None, :, None], 0.0, MASKED).astype(jnp.float32)
    group_rows = shards * rows * dec_heads
    parts = pl.pallas_call(
        dec_attn_kernel,
        out_shape=jax.ShapeDtypeStruct((group_rows, KV_RANK + 128), jnp.bfloat16),
        compiler_params=pltpu.CompilerParams(vmem_limit_bytes=40 << 20),
        name="decode_attention",
    )(
        group_q.reshape(group_rows, width),
        line_kv.reshape(4 * block, width),
        line_bias.reshape(1, 4 * block),
    )
    parts = lax.all_to_all(
        parts.reshape(shards, rows * dec_heads, KV_RANK + 128), SHARDS, 0, 0, tiled=True
    )
    dec_latent = pl.pallas_call(
        combine_kernel,
        out_shape=jax.ShapeDtypeStruct((rows * dec_heads, KV_RANK), jnp.bfloat16),
        name="combine_shards",
    )(parts)

    all_latent = spread(dec_latent, CTX).reshape(ctx_size * rows, dec_heads * KV_RANK)
    cols = w_attn_out.shape[2]
    partial_attn = jnp.dot(
        all_latent, w_attn_out.reshape(dec_heads * KV_RANK, cols), preferred_element_type=jnp.float32
    ).astype(jnp.bfloat16)
    partial_attn = jnp.broadcast_to(
        partial_attn.reshape(ctx_size, 1, rows, cols), (ctx_size, 4, rows, cols)
    ).reshape(ctx_size * 4, rows, cols)
    partial_attn = lax.all_to_all(partial_attn, CTX + HEAD, 0, 0, tiled=True)
    partial_attn = partial_attn.reshape(ctx_size, 4, rows, cols)
    partial_attn = lax.dynamic_slice_in_dim(partial_attn, my_quarter * (ctx_size // 4), ctx_size // 4, 0)
    attn_out = jnp.sum(partial_attn.astype(jnp.float32), axis=1).astype(jnp.bfloat16)
    attn_out = jnp.swapaxes(attn_out, 0, 1).reshape(rows, quarter)
    hidden_quarter = lax.dynamic_slice_in_dim(decode_hidden, my_quarter * quarter, quarter, 1)
    state = (hidden_quarter.astype(jnp.float32) + attn_out.astype(jnp.float32)).astype(jnp.bfloat16)

    experts = jnp.arange(ctx_size, dtype=jnp.int32)
    hits = routes[..., None] == experts
    used = jnp.any(hits, axis=2)
    weight = jnp.sum(jnp.where(hits, gate_weights[..., None], 0.0), axis=2)
    counted = used.astype(jnp.int32)
    earlier = jnp.cumsum(counted, axis=1) - counted
    placed = used[..., None] & (earlier[..., None] == jnp.arange(SLOTS, dtype=jnp.int32))
    dispatch = jnp.moveaxis(placed, 1, -1).astype(jnp.bfloat16)
    dispatch = dispatch.reshape(STEPS, ctx_size * SLOTS, rows)
    collect = jnp.where(placed, weight[..., None], 0.0)
    collect = jnp.broadcast_to(collect[:, :, :, None, :], (STEPS, rows, ctx_size, 2, SLOTS))
    collect = collect.reshape(STEPS, rows, ctx_size * 2 * SLOTS)

    other_cols = lax.dynamic_slice_in_dim(w_down[0], (1 - core) * (model // 2), model // 2, 1)
    w_other = shift(other_cols, "core", 1)
    core_arr = core.astype(jnp.int32).reshape(1)
    gain = norm_gain.reshape(1, model)

    for step in range(STEPS):
        outgoing = jnp.dot(dispatch[step], state, preferred_element_type=jnp.float32)
        outgoing = outgoing.astype(jnp.bfloat16).reshape(ctx_size, 1, SLOTS, quarter)
        outgoing = jnp.broadcast_to(outgoing, (ctx_size, 2, SLOTS, quarter))
        received = lax.all_to_all(
            outgoing.reshape(ctx_size * 2, SLOTS, quarter), LANE, 0, 0, tiled=True
        )
        received = received.reshape(ctx_size, 2, SLOTS, quarter)
        received = jnp.swapaxes(received, 1, 2).reshape(ctx_size * SLOTS, 2 * quarter)
        received = lax.all_gather(received, "core", axis=0)
        inner = expert_inner(received, gain, w_gate[0], w_up[0])
        inner = lax.all_gather(inner, "core", axis=0)
        partial_out = expert_down(core_arr, inner, w_down[0], w_other)
        partial_out = partial_out.reshape(ctx_size, SLOTS, 2, quarter)
        partial_out = jnp.swapaxes(partial_out, 1, 2).reshape(ctx_size * 2, SLOTS, quarter)
        returned = lax.all_to_all(partial_out, LANE, 0, 0, tiled=True)
        returned = returned.reshape(ctx_size * 2 * SLOTS, quarter).astype(jnp.float32)
        added = jnp.dot(
            collect[step], returned, precision=lax.Precision.HIGHEST, preferred_element_type=jnp.float32
        )
        state = (state.astype(jnp.float32) + added).astype(jnp.bfloat16)
    decode_out = lax.all_gather(state, HEAD, axis=0)
    decode_out = decode_out.reshape(2, 2, rows, quarter).transpose(2, 1, 0, 3).reshape(rows, model)

    gathered = lax.all_gather(mine, CTX, axis=0)
    others = shift(gathered, "core", 1)
    at = jnp.arange(half, dtype=jnp.int32)[None, :]

    def bias_of(which):
        return jnp.where(at + which * half < doc_lengths[:, None], 0.0, MASKED).astype(jnp.float32)

    stretch_latent = prefill(
        stretch_queries.reshape(tokens * heads, width),
        gathered.reshape(ctx_size * half, width),
        others.reshape(ctx_size * half, width),
        bias_of(core).reshape(1, ctx_size * half),
        bias_of(1 - core).reshape(1, ctx_size * half),
    )
    return stretch_latent.reshape(tokens, heads, KV_RANK), decode_out


def solution(mesh):
    names = [name for axis in mesh.axis_names for name, _ in SPLIT[axis]]
    sizes = [size for axis in mesh.axis_names for _, size in SPLIT[axis]]
    fine = Mesh(mesh.devices.reshape(sizes), names)
    return jax.shard_map(
        per_device,
        mesh=fine,
        in_specs=(
            P(CTX, HEAD, None),
            P(CTX, None),
            P(),
            P(CTX, HEAD, None),
            P(HEAD, None, CTX),
            P(CTX, None),
            P(),
            P(CTX, None, HEAD),
            P(CTX, None, HEAD),
            P(CTX, HEAD, None),
            P(None, CTX, None),
            P(None, CTX, None),
        ),
        out_specs=(P(CTX, HEAD, None), P(CTX, None)),
        check_vma=False,
    )
```

```python
import functools

import jax
import jax.numpy as jnp
from jax import lax
from jax.experimental import pallas as pl
from jax.experimental.pallas import tpu as pltpu
from jax.sharding import Mesh, PartitionSpec as P

KV_RANK = 512
STEPS = 3
SLOTS = 2
SCALE = 0.07216878364870322
MASKED = -1e30

SPLIT = {"ctx": (("x_lo", 2), ("z", 4), ("y", 4)), "head": (("x_hi", 2), ("core", 2))}
CTX = ("x_lo", "z", "y")
HEAD = ("x_hi", "core")
SHARDS = ("x_lo", "z")
LANE = CTX + ("x_hi",)


def shift(x, axis, by):
    n = lax.axis_size(axis)
    return lax.ppermute(x, axis, [(i, (i + by) % n) for i in range(n)])


def spread(x, axes):
    n = lax.axis_size(axes)
    return lax.all_to_all(jnp.broadcast_to(x[None], (n,) + x.shape), axes, 0, 0, tiled=True)


def dot_t(a, b):
    return lax.dot_general(a, b, (((1,), (1,)), ((), ())), preferred_element_type=jnp.float32)


def tie(x, after):
    anywhere = pl.BlockSpec(memory_space=pl.ANY)
    return pl.pallas_call(
        lambda x_ref, after_ref, out_ref: None,
        in_specs=[anywhere, anywhere],
        out_specs=anywhere,
        out_shape=jax.ShapeDtypeStruct(x.shape, x.dtype),
        input_output_aliases={0: 0},
        compiler_params=pltpu.CompilerParams(vmem_limit_bytes=56 << 20),
        cost_estimate=pl.CostEstimate(flops=0, bytes_accessed=0, transcendentals=0),
        name="tie",
    )(x, after)


def take(ref, at):
    return [ref[i] for i in at]


def dec_attn_kernel(q_ref, own_ref, other_ref, bias_ref, out_ref):
    n = own_ref.shape[0]
    keys = jnp.concatenate(take(own_ref, range(n)) + take(other_ref, range(n)), axis=1)
    s = jnp.dot(q_ref[...], keys, preferred_element_type=jnp.float32) * SCALE + bias_ref[...]
    top = jnp.max(s, axis=1, keepdims=True)
    p = jnp.exp(s - top)
    total = jnp.sum(p, axis=1, keepdims=True)
    acc = dot_t(p.astype(jnp.bfloat16), keys[:KV_RANK])
    out_ref[:, :KV_RANK] = (acc / total).astype(jnp.bfloat16)
    lse = jnp.broadcast_to(top + jnp.log(total), (q_ref.shape[0], 128))
    hi = lse.astype(jnp.bfloat16).astype(jnp.float32)
    mid = (lse - hi).astype(jnp.bfloat16).astype(jnp.float32)
    low = lse - hi - mid
    lane = lax.broadcasted_iota(jnp.int32, lse.shape, 1)
    out_ref[:, KV_RANK:] = jnp.where(
        lane == 0, hi, jnp.where(lane == 1, mid, jnp.where(lane == 2, low, 0.0))
    ).astype(jnp.bfloat16)


def decode_attention(q, own, other, bias):
    rows, width = q.shape
    return pl.pallas_call(
        dec_attn_kernel,
        out_shape=jax.ShapeDtypeStruct((rows, KV_RANK + 128), jnp.bfloat16),
        compiler_params=pltpu.CompilerParams(vmem_limit_bytes=16 << 20),
        cost_estimate=pl.CostEstimate(
            flops=2 * rows * bias.shape[1] * (width + KV_RANK),
            bytes_accessed=4 * rows * width,
            transcendentals=rows * bias.shape[1],
        ),
        name="decode_attention",
    )(q, own, other, bias)


def combine_kernel(parts_ref, out_ref):
    n, rows, _ = parts_ref.shape
    lses = [
        jnp.sum(parts_ref[i, :, KV_RANK:].astype(jnp.float32), axis=1, keepdims=True)
        for i in range(n)
    ]
    top = functools.reduce(jnp.maximum, lses)
    shares = [jnp.exp(x - top) for x in lses]
    total = functools.reduce(jnp.add, shares)
    acc = sum(shares[i] * parts_ref[i, :, :KV_RANK].astype(jnp.float32) for i in range(n))
    out_ref[...] = (acc / total).astype(jnp.bfloat16)


def project_kernel(sides_ref, lat_ref, own_ref, other_ref, keep_ref, send_ref):
    heads, _, rank = own_ref.shape
    own = other = None
    for h in range(heads):
        lat = lat_ref[:, h * rank : (h + 1) * rank]
        mine, theirs = dot_t(lat, own_ref[h]), dot_t(lat, other_ref[h])
        own = mine if own is None else own + mine
        other = theirs if other is None else other + theirs
    same = sides_ref[0] == sides_ref[1]
    keep_ref[...] = jnp.where(same, own, other)
    send_ref[...] = jnp.where(same, other, own).astype(jnp.bfloat16)


def project(sides, latent, w_own, w_other):
    rows, depth = latent.shape
    heads, cols, rank = w_other.shape
    whole = pl.BlockSpec((rows, cols), lambda i, sides: (0, 0))
    return pl.pallas_call(
        project_kernel,
        grid_spec=pltpu.PrefetchScalarGridSpec(
            num_scalar_prefetch=1,
            grid=(1,),
            in_specs=[
                pl.BlockSpec((rows, depth), lambda i, sides: (0, 0)),
                pl.BlockSpec((heads, cols, rank), lambda i, sides: (sides[0], 0, 0)),
                pl.BlockSpec((heads, cols, rank), lambda i, sides: (0, 0, 0)),
            ],
            out_specs=[whole, whole],
        ),
        out_shape=[
            jax.ShapeDtypeStruct((rows, cols), jnp.float32),
            jax.ShapeDtypeStruct((rows, cols), jnp.bfloat16),
        ],
        compiler_params=pltpu.CompilerParams(vmem_limit_bytes=20 << 20),
        cost_estimate=pl.CostEstimate(
            flops=4 * rows * depth * cols, bytes_accessed=4 * depth * cols, transcendentals=0
        ),
        name="project",
    )(sides, latent, w_own, w_other)


def prefill_kernel(q_ref, own_ref, other_ref, bias_ref, *rest):
    out_ref, done_ref, top_ref, total_ref, acc_ref = rest[-5:]
    step = pl.program_id(0)

    @pl.when(step == 0)
    def _():
        top_ref[...] = jnp.full_like(top_ref, MASKED)
        total_ref[...] = jnp.zeros_like(total_ref)
        acc_ref[...] = jnp.zeros_like(acc_ref)
        done_ref[...] = jnp.zeros_like(done_ref)

    n = own_ref.shape[0]
    keys = jnp.concatenate(take(own_ref, range(n)) + take(other_ref, range(n)), axis=1)
    s = jnp.dot(q_ref[...], keys, preferred_element_type=jnp.float32) * SCALE + bias_ref[0]
    old = top_ref[...]
    top = jnp.maximum(old, jnp.max(s, axis=1, keepdims=True))
    p = jnp.exp(s - top)
    fade = jnp.exp(old - top)
    total_ref[...] = total_ref[...] * fade + jnp.sum(p, axis=1, keepdims=True)
    acc_ref[...] = acc_ref[...] * fade + dot_t(p.astype(jnp.bfloat16), keys[:KV_RANK])
    top_ref[...] = top

    @pl.when(step == pl.num_programs(0) - 1)
    def _():
        out_ref[...] = (acc_ref[...] / total_ref[...]).astype(jnp.bfloat16)


def prefill(piece, pieces, q, own, other, bias, after, so_far):
    rows, width = q.shape
    part = rows // pieces
    count = own.shape[0]
    group = 4
    positions = 2 * group * own.shape[2]
    kv_spec = pl.BlockSpec((group,) + own.shape[1:], lambda i: (i, 0, 0))
    anywhere = pl.BlockSpec(memory_space=pl.ANY)
    extra = [after] + ([] if so_far is None else [so_far])
    return pl.pallas_call(
        prefill_kernel,
        grid=(count // group,),
        in_specs=[
            pl.BlockSpec((part, width), lambda i: (piece, 0)),
            kv_spec,
            kv_spec,
            pl.BlockSpec((1, 1, positions), lambda i: (i, 0, 0)),
        ]
        + [anywhere] * len(extra),
        out_specs=[
            pl.BlockSpec((part, KV_RANK), lambda i: (piece, 0)),
            pl.BlockSpec((8, 128), lambda i: (0, 0)),
        ],
        out_shape=[
            jax.ShapeDtypeStruct((rows, KV_RANK), jnp.bfloat16),
            jax.ShapeDtypeStruct((8, 128), jnp.float32),
        ],
        input_output_aliases={} if so_far is None else {5: 0},
        scratch_shapes=[
            pltpu.VMEM((part, 1), jnp.float32),
            pltpu.VMEM((part, 1), jnp.float32),
            pltpu.VMEM((part, KV_RANK), jnp.float32),
        ],
        compiler_params=pltpu.CompilerParams(vmem_limit_bytes=56 << 20),
        cost_estimate=pl.CostEstimate(
            flops=4 * part * count * own.shape[2] * (width + KV_RANK),
            bytes_accessed=4 * count * own.shape[2] * width,
            transcendentals=2 * part * count * own.shape[2],
        ),
        name="prefill",
    )(q, own, other, bias, *extra)


def inner_kernel(x_ref, gain_ref, gate_ref, up_ref, out_ref, x_scr, gate_acc, up_acc):
    cores, pieces, slots, quarter = x_ref.shape
    steps, _, chunk = x_scr.shape
    step = pl.program_id(0)

    @pl.when(step == 0)
    def _():
        square = 0.0
        for core in range(cores):
            for x_hi in range(2):
                x = jnp.concatenate(
                    [x_ref[core, piece].astype(jnp.float32) for piece in range(x_hi, pieces, 2)], axis=0
                )
                square = square + jnp.sum(x * x, axis=1, keepdims=True)
                for part in range(quarter // chunk):
                    x_scr[(core * 2 + x_hi) * (quarter // chunk) + part] = x[:, part * chunk : (part + 1) * chunk].astype(jnp.bfloat16)
        scale = lax.rsqrt(square / (steps * chunk) + 1e-06)
        for part in range(steps):
            x = x_scr[part].astype(jnp.float32) * scale * gain_ref[:, part * chunk : (part + 1) * chunk]
            x_scr[part] = x.astype(jnp.bfloat16)
        gate_acc[...] = jnp.zeros_like(gate_acc)
        up_acc[...] = jnp.zeros_like(up_acc)

    x = x_scr[step]
    gate_acc[...] += jnp.dot(x, gate_ref[...], preferred_element_type=jnp.float32)
    up_acc[...] += jnp.dot(x, up_ref[...], preferred_element_type=jnp.float32)

    @pl.when(step == pl.num_programs(0) - 1)
    def _():
        out_ref[...] = (jax.nn.silu(gate_acc[...]) * up_acc[...]).astype(jnp.bfloat16)


def expert_inner(x, gain, w_gate, w_up):
    rows, (depth, hidden) = x.shape[1] // 2 * x.shape[2], w_gate.shape
    chunk = 896
    w_spec = pl.BlockSpec((chunk, hidden), lambda i: (i, 0))
    return pl.pallas_call(
        inner_kernel,
        grid=(depth // chunk,),
        in_specs=[
            pl.BlockSpec(x.shape, lambda i: (0, 0, 0, 0)),
            pl.BlockSpec((1, depth), lambda i: (0, 0)),
            w_spec,
            w_spec,
        ],
        out_specs=pl.BlockSpec((rows, hidden), lambda i: (0, 0)),
        out_shape=jax.ShapeDtypeStruct((rows, hidden), jnp.bfloat16),
        scratch_shapes=[
            pltpu.VMEM((depth // chunk, rows, chunk), jnp.bfloat16),
            pltpu.VMEM((rows, hidden), jnp.float32),
            pltpu.VMEM((rows, hidden), jnp.float32),
        ],
        compiler_params=pltpu.CompilerParams(vmem_limit_bytes=56 << 20),
        cost_estimate=pl.CostEstimate(
            flops=4 * rows * depth * hidden, bytes_accessed=4 * depth * hidden, transcendentals=rows * hidden
        ),
        name="expert_inner",
    )(x, gain, w_gate, w_up)


def down_kernel(core_ref, inner_ref, own_ref, other_ref, out_ref):
    core = core_ref[0]
    out_ref[...] = (
        jnp.dot(inner_ref[core], own_ref[...], preferred_element_type=jnp.float32)
        + jnp.dot(inner_ref[1 - core], other_ref[...], preferred_element_type=jnp.float32)
    ).astype(jnp.bfloat16)


def expert_down(core, inner, w_down, w_other):
    _, rows, hidden = inner.shape
    width = w_other.shape[1]
    block = 896
    steps = width // block
    return pl.pallas_call(
        down_kernel,
        grid_spec=pltpu.PrefetchScalarGridSpec(
            num_scalar_prefetch=1,
            grid=(steps,),
            in_specs=[
                pl.BlockSpec(inner.shape, lambda i, core: (0, 0, 0)),
                pl.BlockSpec((hidden, block), lambda i, core: (0, core[0] * steps + i)),
                pl.BlockSpec((hidden, block), lambda i, core: (0, i)),
            ],
            out_specs=pl.BlockSpec((rows, block), lambda i, core: (0, i)),
        ),
        out_shape=jax.ShapeDtypeStruct((rows, width), jnp.bfloat16),
        compiler_params=pltpu.CompilerParams(vmem_limit_bytes=56 << 20),
        cost_estimate=pl.CostEstimate(
            flops=4 * rows * hidden * width, bytes_accessed=4 * hidden * width, transcendentals=0
        ),
        name="expert_down",
    )(core, inner, w_down, w_other)


def collect_kernel(weight_ref, returned_ref, state_ref, *rest):
    out_ref = rest[-1]
    added = jnp.dot(
        weight_ref[...],
        returned_ref[...].astype(jnp.float32),
        precision=lax.Precision.HIGHEST,
        preferred_element_type=jnp.float32,
    )
    out_ref[...] = (state_ref[...].astype(jnp.float32) + added).astype(jnp.bfloat16)


def collect_rows(weight, returned, state, extra):
    vmem = pl.BlockSpec(memory_space=pltpu.VMEM)
    return pl.pallas_call(
        collect_kernel,
        in_specs=[vmem] * 3 + [pl.BlockSpec(memory_space=pl.ANY)] * len(extra),
        out_specs=vmem,
        out_shape=jax.ShapeDtypeStruct(state.shape, state.dtype),
        compiler_params=pltpu.CompilerParams(vmem_limit_bytes=8 << 20),
        name="collect_rows",
    )(weight, returned, state, *extra)


def per_device(
    stretch_queries,
    cache_latent,
    doc_lengths,
    decode_queries,
    w_attn_out,
    decode_hidden,
    norm_gain,
    w_gate,
    w_up,
    w_down,
    routes,
    gate_weights,
):
    tokens, heads, width = stretch_queries.shape
    rows, dec_heads, _ = decode_queries.shape
    block = cache_latent.shape[0]
    half = block // 2
    ctx_size = lax.axis_size(CTX)
    model = decode_hidden.shape[1]
    core = lax.axis_index("core")
    x_hi = lax.axis_index("x_hi")
    x_lo = lax.axis_index("x_lo")
    quarter = model // 4
    my_quarter = core * 2 + x_hi

    w_out = jnp.swapaxes(w_attn_out, 1, 2)
    w_out_other = shift(
        lax.dynamic_slice_in_dim(w_out, (1 - x_lo) * (dec_heads // 2), dec_heads // 2, 0), "x_lo", 1
    )

    mine = lax.dynamic_slice_in_dim(cache_latent.T, core * half, half, 1)

    line = jnp.stack([mine] + [shift(mine, "y", by) for by in (1, 3, 2)])
    dec_q = decode_queries.reshape(rows * dec_heads, width)
    group_q = spread(dec_q, SHARDS)
    shards = group_q.shape[0]
    line_other = shift(line, "core", 1)
    y = lax.axis_index("y")
    line_at = lax.axis_index(SHARDS) * 4 + (y - jnp.array([0, 1, 3, 2], jnp.int32)) % 4
    line_len = jnp.sum(
        jnp.where(line_at[:, None] == jnp.arange(doc_lengths.shape[0])[None, :], doc_lengths[None, :], 0), axis=1
    )
    place = jnp.arange(half, dtype=jnp.int32)

    def bias_of(which, lengths):
        usable = place + which * half < lengths[..., None]
        return jnp.where(usable, 0.0, MASKED).astype(jnp.float32)

    line_bias = jnp.stack([bias_of(core, line_len), bias_of(1 - core, line_len)])
    parts = decode_attention(
        group_q.reshape(shards * rows * dec_heads, width), line, line_other, line_bias.reshape(1, 4 * block)
    )
    parts = lax.all_to_all(
        parts.reshape(shards, rows * dec_heads, KV_RANK + 128), SHARDS, 0, 0, tiled=True
    )
    dec_latent = pl.pallas_call(
        combine_kernel,
        out_shape=jax.ShapeDtypeStruct((rows * dec_heads, KV_RANK), jnp.bfloat16),
        compiler_params=pltpu.CompilerParams(vmem_limit_bytes=8 << 20),
        name="combine_shards",
    )(parts)

    depth = dec_heads // 2 * KV_RANK
    latent_halves = jnp.swapaxes(dec_latent.reshape(rows, 2, depth), 0, 1)
    latent_halves = jnp.broadcast_to(latent_halves[:, None], (2, ctx_size // 2, rows, depth))
    all_latent = lax.all_to_all(
        latent_halves.reshape(ctx_size, rows, depth), CTX, 0, 0, tiled=True
    )
    cols = w_out.shape[1]
    sides = jnp.stack([x_lo, core]).astype(jnp.int32)
    keep, send = project(sides, all_latent.reshape(ctx_size * rows, depth), w_out, w_out_other)
    attn_cols = (keep + shift(send, "core", 1).astype(jnp.float32)).astype(jnp.bfloat16)
    attn_cols = jnp.broadcast_to(
        attn_cols.reshape(ctx_size, 1, rows, cols), (ctx_size, 2, rows, cols)
    ).reshape(ctx_size * 2, rows, cols)
    attn_parts = lax.all_to_all(attn_cols, LANE, 0, 0, tiled=True)
    attn_parts = attn_parts.reshape(2, 2, 2, 4, 2, rows, cols)
    attn_parts = lax.dynamic_index_in_dim(attn_parts, x_hi, 1, keepdims=False)
    attn_out = jnp.sum(attn_parts.astype(jnp.float32), axis=(0, 3)).astype(jnp.bfloat16)
    attn_out = jnp.swapaxes(attn_out.reshape(8, rows, cols), 0, 1).reshape(rows, quarter)
    hidden_quarter = lax.dynamic_slice_in_dim(decode_hidden, my_quarter * quarter, quarter, 1)
    state = (hidden_quarter.astype(jnp.float32) + attn_out.astype(jnp.float32)).astype(jnp.bfloat16)

    experts = jnp.arange(ctx_size, dtype=jnp.int32)
    hits = routes[..., None] == experts
    used = jnp.any(hits, axis=2)
    weight = jnp.sum(jnp.where(hits, gate_weights[..., None], 0.0), axis=2)
    counted = used.astype(jnp.int32)
    earlier = jnp.cumsum(counted, axis=1) - counted
    placed = used[..., None] & (earlier[..., None] == jnp.arange(SLOTS, dtype=jnp.int32))
    dispatch = jnp.moveaxis(placed, 1, -1).astype(jnp.bfloat16)
    dispatch = dispatch.reshape(STEPS, ctx_size * SLOTS, rows)
    collect = jnp.where(placed, weight[..., None], 0.0)
    collect = jnp.broadcast_to(collect[:, :, :, None, :], (STEPS, rows, ctx_size, 2, SLOTS))
    collect = collect.reshape(STEPS, rows, ctx_size * 2 * SLOTS)

    other_cols = lax.dynamic_slice_in_dim(w_down[0], (1 - core) * (model // 2), model // 2, 1)
    w_other = shift(other_cols, "core", 1)
    core_arr = core.astype(jnp.int32).reshape(1)
    gain = norm_gain.reshape(1, model)

    line_late = tie(line, dec_latent)
    gathered = lax.all_gather(line_late, SHARDS, axis=0).reshape(ctx_size, width, half)
    gathered_at = (
        jnp.arange(shards, dtype=jnp.int32)[:, None] * 4 + (y - jnp.array([0, 1, 3, 2], jnp.int32)) % 4
    ).reshape(ctx_size)
    gathered_len = jnp.sum(
        jnp.where(gathered_at[:, None] == jnp.arange(ctx_size)[None, :], doc_lengths[None, :], 0), axis=1
    )
    bias = jnp.stack(
        [bias_of(core, gathered_len).reshape(-1, 4, half), bias_of(1 - core, gathered_len).reshape(-1, 4, half)],
        axis=1,
    ).reshape(ctx_size // 4, 1, 8 * half)
    flat_q = stretch_queries.reshape(tokens * heads, width)
    stretch_latent = None

    for step in range(STEPS):
        last = step == STEPS - 1
        outgoing = jnp.dot(dispatch[step], state, preferred_element_type=jnp.float32)
        outgoing = outgoing.astype(jnp.bfloat16).reshape(ctx_size, 1, SLOTS, quarter)
        outgoing = jnp.broadcast_to(outgoing, (ctx_size, 2, SLOTS, quarter))
        outgoing = outgoing.reshape(ctx_size * 2, SLOTS, quarter)
        received = lax.all_to_all(outgoing, LANE, 0, 0, tiled=True)
        if last:
            stretch_latent, token = prefill(0, 2, flat_q, gathered, others, bias, state, None)
            received = tie(received, token)
        received = lax.all_gather(received, "core", axis=0)
        inner = expert_inner(received, gain, w_gate[0], w_up[0])
        inner = lax.all_gather(inner, "core", axis=0)
        partial_out = expert_down(core_arr, inner, w_down[0], w_other)
        if step == STEPS - 2:
            gathered = tie(gathered, partial_out)
            others = shift(gathered, "core", 1)
        extra = []
        if last:
            stretch_latent, token = prefill(1, 2, flat_q, gathered, others, bias, partial_out, stretch_latent)
            extra = [token]
        partial_out = partial_out.reshape(ctx_size, SLOTS, 2, quarter)
        partial_out = jnp.swapaxes(partial_out, 1, 2).reshape(ctx_size * 2, SLOTS, quarter)
        returned = lax.all_to_all(partial_out, LANE, 0, 0, tiled=True)
        returned = returned.reshape(ctx_size * 2 * SLOTS, quarter)
        state = collect_rows(collect[step], returned, state, extra)
    decode_out = lax.all_gather(state, HEAD, axis=0)
    decode_out = decode_out.reshape(2, 2, rows, quarter).transpose(2, 1, 0, 3).reshape(rows, model)
    return stretch_latent.reshape(tokens, heads, KV_RANK), decode_out


def solution(mesh):
    names = [name for axis in mesh.axis_names for name, _ in SPLIT[axis]]
    sizes = [size for axis in mesh.axis_names for _, size in SPLIT[axis]]
    fine = Mesh(mesh.devices.reshape(sizes), names)
    return jax.shard_map(
        per_device,
        mesh=fine,
        in_specs=(
            P(CTX, HEAD, None),
            P(CTX, None),
            P(),
            P(CTX, HEAD, None),
            P(HEAD, None, CTX),
            P(CTX, None),
            P(),
            P(CTX, None, HEAD),
            P(CTX, None, HEAD),
            P(CTX, HEAD, None),
            P(None, CTX, None),
            P(None, CTX, None),
        ),
        out_specs=(P(CTX, HEAD, None), P(CTX, None)),
        check_vma=False,
    )
```

```python
import functools

import jax
import jax.numpy as jnp
from jax import lax
from jax.experimental import pallas as pl
from jax.experimental.pallas import tpu as pltpu
from jax.sharding import Mesh, PartitionSpec as P

KV_RANK = 512
STEPS = 3
SLOTS = 2
SCALE = 0.07216878364870322
MASKED = -1e30
KV_ARRAYS = 2
PIECES = 2 * STEPS - 2
TURNS = (0, 1, 3, 2)
BIG_VMEM = 56 << 20
EXPERT_VMEM = 50 << 20
AHEAD = 3

SPLIT = {"ctx": (("x_lo", 2), ("z", 4), ("y", 4)), "head": (("x_hi", 2), ("core", 2))}
CTX = ("x_lo", "z", "y")
HEAD = ("x_hi", "core")
SHARDS = "z"
LANE = CTX + ("x_hi",)


def shift(x, axis, by):
    n = lax.axis_size(axis)
    return lax.ppermute(x, axis, [(i, (i + by) % n) for i in range(n)])


def spread(x, axes):
    n = lax.axis_size(axes)
    return lax.all_to_all(jnp.broadcast_to(x[None], (n,) + x.shape), axes, 0, 0, tiled=True)


def dot_t(a, b):
    return lax.dot_general(a, b, (((1,), (1,)), ((), ())), preferred_element_type=jnp.float32)


def tie(x, *after, vmem=None):
    anywhere = pl.BlockSpec(memory_space=pl.ANY)
    return pl.pallas_call(
        lambda *refs: None,
        in_specs=[anywhere] * (1 + len(after)),
        out_specs=anywhere,
        out_shape=jax.ShapeDtypeStruct(x.shape, x.dtype),
        input_output_aliases={0: 0},
        compiler_params=pltpu.CompilerParams(vmem_limit_bytes=vmem or BIG_VMEM),
        cost_estimate=pl.CostEstimate(flops=0, bytes_accessed=0, transcendentals=0),
        name="tie",
    )(x, *after)


def take(ref, at):
    return [ref[i] for i in at]


def dec_attn_kernel(q_ref, own_ref, other_ref, bias_ref, out_ref):
    n = own_ref.shape[0]
    keys = jnp.concatenate(take(own_ref, range(n)) + take(other_ref, range(n)), axis=1)
    s = jnp.dot(q_ref[...], keys, preferred_element_type=jnp.float32) * SCALE + bias_ref[...]
    top = jnp.max(s, axis=1, keepdims=True)
    p = jnp.exp(s - top)
    total = jnp.sum(p, axis=1, keepdims=True)
    acc = dot_t(p.astype(jnp.bfloat16), keys[:KV_RANK])
    out_ref[:, :KV_RANK] = (acc / total).astype(jnp.bfloat16)
    lse = jnp.broadcast_to(top + jnp.log(total), (q_ref.shape[0], 128))
    hi = lse.astype(jnp.bfloat16).astype(jnp.float32)
    mid = (lse - hi).astype(jnp.bfloat16).astype(jnp.float32)
    low = lse - hi - mid
    lane = lax.broadcasted_iota(jnp.int32, lse.shape, 1)
    out_ref[:, KV_RANK:] = jnp.where(
        lane == 0, hi, jnp.where(lane == 1, mid, jnp.where(lane == 2, low, 0.0))
    ).astype(jnp.bfloat16)


def decode_attention(q, own, other, bias):
    rows, width = q.shape
    return pl.pallas_call(
        dec_attn_kernel,
        out_shape=jax.ShapeDtypeStruct((rows, KV_RANK + 128), jnp.bfloat16),
        compiler_params=pltpu.CompilerParams(vmem_limit_bytes=16 << 20),
        cost_estimate=pl.CostEstimate(
            flops=2 * rows * bias.shape[1] * (width + KV_RANK),
            bytes_accessed=4 * rows * width,
            transcendentals=rows * bias.shape[1],
        ),
        name="decode_attention",
    )(q, own, other, bias)


def combine_kernel(parts_ref, out_ref):
    n, rows, _ = parts_ref.shape
    lses = [
        jnp.sum(parts_ref[i, :, KV_RANK:].astype(jnp.float32), axis=1, keepdims=True)
        for i in range(n)
    ]
    top = functools.reduce(jnp.maximum, lses)
    shares = [jnp.exp(x - top) for x in lses]
    total = functools.reduce(jnp.add, shares)
    acc = sum(shares[i] * parts_ref[i, :, :KV_RANK].astype(jnp.float32) for i in range(n))
    out_ref[...] = (acc / total).astype(jnp.bfloat16)


def project_kernel(lat_ref, w_ref, out_ref):
    heads, _, rank = w_ref.shape
    total = None
    for h in range(heads):
        part = dot_t(lat_ref[:, h * rank : (h + 1) * rank], w_ref[h])
        total = part if total is None else total + part
    out_ref[...] = total.astype(jnp.bfloat16)


def project(latent, w_out):
    rows, depth = latent.shape
    heads, cols, rank = w_out.shape
    return pl.pallas_call(
        project_kernel,
        out_shape=jax.ShapeDtypeStruct((rows, cols), jnp.bfloat16),
        compiler_params=pltpu.CompilerParams(vmem_limit_bytes=20 << 20),
        cost_estimate=pl.CostEstimate(
            flops=2 * rows * depth * cols, bytes_accessed=2 * depth * cols, transcendentals=0
        ),
        name="project",
    )(latent, w_out)


def prefill_kernel(piece, pieces, q_ref, bias_ref, own_hbm, other_hbm, after, *rest):
    own_buf, other_buf, acc_buf, sems, acc_sem = rest[-5:]
    steps, group, _, _ = own_buf.shape
    rows = q_ref.shape[0]

    def copies(i):
        at = pl.ds((piece * steps + i) * group, group)
        return (
            pltpu.make_async_copy(own_hbm.at[at], own_buf.at[i], sems.at[0, i]),
            pltpu.make_async_copy(other_hbm.at[at], other_buf.at[i], sems.at[1, i]),
        )

    for i in range(steps):
        for copy in copies(i):
            copy.start()
    if piece > 0:
        acc_copy = pltpu.make_async_copy(rest[0], acc_buf, acc_sem)
        acc_copy.start()
    q = q_ref[...]
    top = total = acc = None
    for i in range(steps):
        for copy in copies(i):
            copy.wait()
        keys = jnp.concatenate(take(own_buf.at[i], range(group)) + take(other_buf.at[i], range(group)), axis=1)
        s = jnp.dot(q, keys, preferred_element_type=jnp.float32) * SCALE + bias_ref[i]
        best = jnp.max(s, axis=1, keepdims=True)
        new = best if top is None else jnp.maximum(top, best)
        p = jnp.exp(s - new)
        p_sum = jnp.sum(p, axis=1, keepdims=True)
        part = dot_t(p.astype(jnp.bfloat16), keys[:KV_RANK])
        if top is None:
            total, acc = p_sum, part
        else:
            fade = jnp.exp(top - new)
            total, acc = total * fade + p_sum, acc * fade + part
        top = new
    if piece > 0:
        old, old_total = rest[1][:, 0:1], rest[1][:, 1:2]
        new = jnp.maximum(top, old)
        fade, old_fade = jnp.exp(top - new), jnp.exp(old - new)
        acc_copy.wait()
        total = total * fade + old_total * old_fade
        acc = acc * fade + acc_buf[...] * old_fade
        top = new
        rest = rest[2:]
    if piece == pieces - 1:
        rest[0][...] = (acc / total).astype(jnp.bfloat16)
        rest[1][...] = jnp.zeros_like(rest[1])
    else:
        rest[0][...] = acc
        lane = lax.broadcasted_iota(jnp.int32, rest[1].shape, 1)
        rest[1][...] = jnp.where(lane == 0, top, total)


def prefill(piece, pieces, q, bias, own, other, after, so_far):
    rows, width = q.shape
    blocks, _, half = own.shape
    steps, _, positions = bias.shape
    steps //= pieces
    whole = pl.BlockSpec((rows, KV_RANK), lambda i: (0, 0))
    stats = pl.BlockSpec((rows, 128), lambda i: (0, 0))
    last = piece == pieces - 1
    anywhere = pl.BlockSpec(memory_space=pl.ANY)
    buf = pltpu.VMEM((steps, blocks // pieces // steps, width, half), jnp.bfloat16)
    return pl.pallas_call(
        functools.partial(prefill_kernel, piece, pieces),
        grid=(1,),
        in_specs=[
            pl.BlockSpec((rows, width), lambda i: (0, 0)),
            pl.BlockSpec((steps, 1, positions), lambda i: (piece, 0, 0)),
            anywhere,
            anywhere,
            anywhere,
        ]
        + ([anywhere, stats] if so_far else []),
        out_specs=[whole, stats],
        out_shape=[
            jax.ShapeDtypeStruct((rows, KV_RANK), jnp.bfloat16 if last else jnp.float32),
            jax.ShapeDtypeStruct((rows, 128), jnp.float32),
        ],
        scratch_shapes=[
            buf,
            buf,
            pltpu.VMEM((rows, KV_RANK), jnp.float32),
            pltpu.SemaphoreType.DMA((2, steps)),
            pltpu.SemaphoreType.DMA,
        ],
        compiler_params=pltpu.CompilerParams(vmem_limit_bytes=BIG_VMEM),
        cost_estimate=pl.CostEstimate(
            flops=2 * rows * steps * positions * (width + KV_RANK),
            bytes_accessed=2 * steps * positions * width,
            transcendentals=rows * steps * positions,
        ),
        name="prefill",
    )(q, bias, own, other, after, *so_far)


def expert_kernel(
    core_ref, x_ref, gain_ref, gate_hbm, up_hbm, down_hbm, keep_ref, send_ref, gate_buf, up_buf, down_buf, sems, down_sems
):
    halves, _, width = x_ref.shape
    parts, chunk, _ = gate_buf.shape
    core = core_ref[0]

    def copies(i):
        rows = pl.ds(i * chunk, chunk)
        return (
            pltpu.make_async_copy(gate_hbm.at[rows, :], gate_buf.at[i], sems.at[0, i]),
            pltpu.make_async_copy(up_hbm.at[rows, :], up_buf.at[i], sems.at[1, i]),
        )

    def down_copy(i):
        return pltpu.make_async_copy(
            down_hbm.at[:, pl.ds(i * chunk, chunk)], down_buf.at[i], down_sems.at[i]
        )

    def start(i):
        if i < parts:
            for copy in copies(i):
                copy.start()
        elif i < 2 * parts:
            down_copy(i - parts).start()

    for i in range(AHEAD):
        start(i)
    square = 0.0
    for half in range(halves):
        x = x_ref[half].astype(jnp.float32)
        square = square + jnp.sum(x * x, axis=1, keepdims=True)
    scale = lax.rsqrt(square / (halves * width) + 1e-06)
    gate = up = None
    for i in range(parts):
        half, at = divmod(i * chunk, width)
        x = x_ref[half, :, at : at + chunk].astype(jnp.float32) * scale
        x = (x * gain_ref[:, i * chunk : (i + 1) * chunk]).astype(jnp.bfloat16)
        for copy in copies(i):
            copy.wait()
        start(i + AHEAD)
        g = jnp.dot(x, gate_buf[i], preferred_element_type=jnp.float32)
        u = jnp.dot(x, up_buf[i], preferred_element_type=jnp.float32)
        gate = g if gate is None else gate + g
        up = u if up is None else up + u
    inner = (jax.nn.silu(gate) * up).astype(jnp.bfloat16)
    for i in range(parts):
        down_copy(i).wait()
        start(parts + i + AHEAD)
        out = jnp.dot(inner, down_buf[i], preferred_element_type=jnp.float32).astype(jnp.bfloat16)
        half, at = divmod(i * chunk, width)

        @pl.when(core == half)
        def _():
            keep_ref[:, at : at + chunk] = out

        @pl.when(core != half)
        def _():
            send_ref[:, at : at + chunk] = out


def expert(core, x, gain, w_gate, w_up, w_down):
    _, rows, width = x.shape
    depth, hidden = w_gate.shape
    chunk = 896
    parts = depth // chunk
    vmem, anywhere = pl.BlockSpec(memory_space=pltpu.VMEM), pl.BlockSpec(memory_space=pl.ANY)
    return pl.pallas_call(
        expert_kernel,
        in_specs=[pl.BlockSpec(memory_space=pltpu.SMEM), vmem, vmem] + [anywhere] * 3,
        out_specs=[vmem, vmem],
        out_shape=[jax.ShapeDtypeStruct((rows, width), jnp.bfloat16)] * 2,
        scratch_shapes=[
            pltpu.VMEM((parts, chunk, hidden), jnp.bfloat16),
            pltpu.VMEM((parts, chunk, hidden), jnp.bfloat16),
            pltpu.VMEM((parts, hidden, chunk), jnp.bfloat16),
            pltpu.SemaphoreType.DMA((2, parts)),
            pltpu.SemaphoreType.DMA((parts,)),
        ],
        compiler_params=pltpu.CompilerParams(vmem_limit_bytes=EXPERT_VMEM),
        cost_estimate=pl.CostEstimate(
            flops=6 * rows * depth * hidden, bytes_accessed=6 * depth * hidden, transcendentals=rows * hidden
        ),
        name="expert",
    )(core, x, gain, w_gate, w_up, w_down)


def collect_kernel(weight_ref, returned_ref, state_ref, *rest):
    out_ref = rest[-1]
    added = jnp.dot(
        weight_ref[...],
        returned_ref[...].astype(jnp.float32),
        precision=lax.Precision.HIGHEST,
        preferred_element_type=jnp.float32,
    )
    out_ref[...] = (state_ref[...].astype(jnp.float32) + added).astype(jnp.bfloat16)


def collect_rows(weight, returned, state, extra):
    vmem = pl.BlockSpec(memory_space=pltpu.VMEM)
    return pl.pallas_call(
        collect_kernel,
        in_specs=[vmem] * 3 + [pl.BlockSpec(memory_space=pl.ANY)] * len(extra),
        out_specs=vmem,
        out_shape=jax.ShapeDtypeStruct(state.shape, state.dtype),
        compiler_params=pltpu.CompilerParams(vmem_limit_bytes=8 << 20),
        name="collect_rows",
    )(weight, returned, state, *extra)


def per_device(
    stretch_queries,
    cache_latent,
    doc_lengths,
    decode_queries,
    w_attn_out,
    decode_hidden,
    norm_gain,
    w_gate,
    w_up,
    w_down,
    routes,
    gate_weights,
):
    tokens, heads, width = stretch_queries.shape
    rows, dec_heads, _ = decode_queries.shape
    block = cache_latent.shape[0]
    half = block // 2
    ctx_size = lax.axis_size(CTX)
    model = decode_hidden.shape[1]
    core = lax.axis_index("core")
    x_hi = lax.axis_index("x_hi")
    x_lo = lax.axis_index("x_lo")
    quarter = model // 4
    my_quarter = core * 2 + x_hi

    mine = lax.dynamic_slice_in_dim(cache_latent.T, core * half, half, 1)

    pair = jnp.stack([mine, shift(mine, "x_lo", 1)])
    line = jnp.concatenate([pair] + [shift(pair, "y", by) for by in TURNS[1:]])
    dec_q = decode_queries.reshape(rows * dec_heads, width)
    group_q = spread(dec_q, SHARDS)
    shards = group_q.shape[0]
    line = tie(line, group_q, vmem=8 << 20)
    line_other = shift(line, "core", 1)
    y = lax.axis_index("y")
    z = lax.axis_index("z")
    y_at = (y - jnp.array(TURNS, jnp.int32)) % 4

    def plane_at(z_at):
        return ((x_lo ^ jnp.arange(2, dtype=jnp.int32)) * 4 + z_at) * 4 + y_at[:, None]

    def lengths_of(blocks):
        hit = blocks[..., None] == jnp.arange(doc_lengths.shape[0], dtype=jnp.int32)
        return jnp.sum(jnp.where(hit, doc_lengths, 0), axis=-1)

    line_len = lengths_of(plane_at(z).reshape(8))
    place = jnp.arange(half, dtype=jnp.int32)

    def bias_of(which, lengths):
        usable = place + which * half < lengths[..., None]
        return jnp.where(usable, 0.0, MASKED).astype(jnp.float32)

    line_bias = jnp.stack([bias_of(core, line_len), bias_of(1 - core, line_len)])
    parts = decode_attention(
        group_q.reshape(shards * rows * dec_heads, width), line, line_other, line_bias.reshape(1, 8 * block)
    )
    parts = lax.all_to_all(
        parts.reshape(shards, rows * dec_heads, KV_RANK + 128), SHARDS, 0, 0, tiled=True
    )
    dec_latent = pl.pallas_call(
        combine_kernel,
        out_shape=jax.ShapeDtypeStruct((rows * dec_heads, KV_RANK), jnp.bfloat16),
        compiler_params=pltpu.CompilerParams(vmem_limit_bytes=8 << 20),
        name="combine_shards",
    )(parts)

    all_latent = spread(dec_latent.reshape(rows, dec_heads * KV_RANK), CTX)
    cols = w_attn_out.shape[2]
    partial_attn = project(
        all_latent.reshape(ctx_size * rows, dec_heads * KV_RANK), jnp.swapaxes(w_attn_out, 1, 2)
    )
    both = lax.all_gather(partial_attn, "core", axis=0)
    attn_cols = jnp.sum(both.astype(jnp.float32), axis=0).astype(jnp.bfloat16)
    attn_cols = jnp.broadcast_to(
        attn_cols.reshape(ctx_size, 1, rows, cols), (ctx_size, 2, rows, cols)
    ).reshape(ctx_size * 2, rows, cols)
    attn_parts = lax.all_to_all(attn_cols, LANE, 0, 0, tiled=True)
    attn_parts = attn_parts.reshape(4, ctx_size // 4, 2, rows, cols)
    attn_parts = lax.dynamic_index_in_dim(attn_parts, my_quarter, 0, keepdims=False)
    attn_out = jnp.sum(attn_parts.astype(jnp.float32), axis=1).astype(jnp.bfloat16)
    attn_out = jnp.swapaxes(attn_out.reshape(8, rows, cols), 0, 1).reshape(rows, quarter)
    hidden_quarter = lax.dynamic_slice_in_dim(decode_hidden, my_quarter * quarter, quarter, 1)
    state = (hidden_quarter.astype(jnp.float32) + attn_out.astype(jnp.float32)).astype(jnp.bfloat16)

    experts = jnp.arange(ctx_size, dtype=jnp.int32)
    hits = routes[..., None] == experts
    used = jnp.any(hits, axis=2)
    weight = jnp.sum(jnp.where(hits, gate_weights[..., None], 0.0), axis=2)
    counted = used.astype(jnp.int32)
    earlier = jnp.cumsum(counted, axis=1) - counted
    placed = used[..., None] & (earlier[..., None] == jnp.arange(SLOTS, dtype=jnp.int32))
    dispatch = jnp.moveaxis(placed, 1, -1).astype(jnp.bfloat16)
    dispatch = dispatch.reshape(STEPS, ctx_size * SLOTS, rows)
    collect = jnp.where(placed, weight[..., None], 0.0)
    collect = jnp.broadcast_to(collect[:, :, :, None, :], (STEPS, rows, ctx_size, 2, SLOTS))
    collect = collect.reshape(STEPS, rows, ctx_size * 2 * SLOTS)

    core_arr = core.astype(jnp.int32).reshape(1)
    gain = norm_gain.reshape(1, model)

    gathered = lax.all_gather(tie(line, all_latent), "z", axis=0, tiled=True)
    all_len = lengths_of(plane_at(jnp.arange(4, dtype=jnp.int32)[:, None, None]).reshape(8, 4))
    bias = jnp.stack([bias_of(core, all_len), bias_of(1 - core, all_len)], axis=1)
    bias = bias.reshape(8, 1, KV_ARRAYS * 4 * half)
    flat_q = stretch_queries.reshape(tokens * heads, width)
    sums = ()

    for step in range(STEPS):
        outgoing = jnp.dot(dispatch[step], state, preferred_element_type=jnp.float32)
        outgoing = outgoing.astype(jnp.bfloat16).reshape(ctx_size, 1, SLOTS, quarter)
        outgoing = jnp.broadcast_to(outgoing, (ctx_size, 2, SLOTS, quarter))
        outgoing = outgoing.reshape(ctx_size * 2, SLOTS, quarter)
        received = lax.all_to_all(outgoing, LANE, 0, 0, tiled=True)
        if step > 0:
            sums = prefill(2 * step - 2, PIECES, flat_q, bias, *kv, state, sums)
            received = tie(received, sums[1])
        received = received.reshape(ctx_size, 2, SLOTS, quarter)
        received = jnp.swapaxes(received, 1, 2).reshape(ctx_size * SLOTS, 2 * quarter)
        received = lax.all_gather(received, "core", axis=0)
        keep, send = expert(core_arr, received, gain, w_gate[0], w_up[0], w_down[0])
        partial_out = (keep.astype(jnp.float32) + shift(send, "core", 1).astype(jnp.float32)).astype(jnp.bfloat16)
        if step == 0:
            gathered = tie(gathered, partial_out)
            kv = [gathered, shift(gathered, "core", 1)]
        extra = []
        if step > 0:
            sums = prefill(2 * step - 1, PIECES, flat_q, bias, *kv, partial_out, sums)
            extra = [sums[1]]
        partial_out = partial_out.reshape(ctx_size, SLOTS, 2, quarter)
        partial_out = jnp.swapaxes(partial_out, 1, 2).reshape(ctx_size * 2, SLOTS, quarter)
        returned = lax.all_to_all(partial_out, LANE, 0, 0, tiled=True)
        returned = returned.reshape(ctx_size * 2 * SLOTS, quarter)
        state = collect_rows(collect[step], returned, state, extra)
    decode_out = lax.all_gather(state, HEAD, axis=0)
    decode_out = decode_out.reshape(2, 2, rows, quarter).transpose(2, 1, 0, 3).reshape(rows, model)
    return sums[0].reshape(tokens, heads, KV_RANK), decode_out


def solution(mesh):
    names = [name for axis in mesh.axis_names for name, _ in SPLIT[axis]]
    sizes = [size for axis in mesh.axis_names for _, size in SPLIT[axis]]
    fine = Mesh(mesh.devices.reshape(sizes), names)
    return jax.shard_map(
        per_device,
        mesh=fine,
        in_specs=(
            P(CTX, HEAD, None),
            P(CTX, None),
            P(),
            P(CTX, HEAD, None),
            P(HEAD, None, CTX),
            P(CTX, None),
            P(),
            P(CTX, None, HEAD),
            P(CTX, None, HEAD),
            P(CTX, HEAD, None),
            P(None, CTX, None),
            P(None, CTX, None),
        ),
        out_specs=(P(CTX, HEAD, None), P(CTX, None)),
        check_vma=False,
    )
```

```python
import functools

import jax
import jax.numpy as jnp
from jax import lax
from jax.experimental import pallas as pl
from jax.experimental.pallas import tpu as pltpu
from jax.sharding import Mesh, PartitionSpec as P

KV_RANK = 512
STEPS = 3
SLOTS = 2
SCALE = 0.07216878364870322
MASKED = -1e30
KV_ARRAYS = 2
PIECES = 2 * STEPS - 2
TURNS = (0, 1, 3, 2)
BIG_VMEM = 56 << 20
EXPERT_VMEM = 50 << 20
AHEAD = 3

SPLIT = {"ctx": (("x_lo", 2), ("z", 4), ("y", 4)), "head": (("x_hi", 2), ("core", 2))}
CTX = ("x_lo", "z", "y")
HEAD = ("x_hi", "core")
SHARDS = "z"
LANE = CTX + ("x_hi",)
X = ("x_lo", "x_hi")


def shift(x, axis, by):
    n = lax.axis_size(axis)
    return lax.ppermute(x, axis, [(i, (i + by) % n) for i in range(n)])


def x_index(x):
    return x % 2 * 2 + x % 4 // 2


def spread(x, axes):
    n = lax.axis_size(axes)
    return lax.all_to_all(jnp.broadcast_to(x[None], (n,) + x.shape), axes, 0, 0, tiled=True)


def dot_t(a, b):
    return lax.dot_general(a, b, (((1,), (1,)), ((), ())), preferred_element_type=jnp.float32)


def tie(x, *after, vmem=None):
    anywhere = pl.BlockSpec(memory_space=pl.ANY)
    return pl.pallas_call(
        lambda *refs: None,
        in_specs=[anywhere] * (1 + len(after)),
        out_specs=anywhere,
        out_shape=jax.ShapeDtypeStruct(x.shape, x.dtype),
        input_output_aliases={0: 0},
        compiler_params=pltpu.CompilerParams(vmem_limit_bytes=vmem or BIG_VMEM),
        cost_estimate=pl.CostEstimate(flops=0, bytes_accessed=0, transcendentals=0),
        name="tie",
    )(x, *after)


def take(ref, at):
    return [ref[i] for i in at]


def dec_attn_kernel(q_ref, *rest):
    bias_ref, out_ref = rest[-2:]
    keys = jnp.concatenate([block for ref in rest[:-2] for block in take(ref, range(ref.shape[0]))], axis=1)
    s = jnp.dot(q_ref[...], keys, preferred_element_type=jnp.float32) * SCALE + bias_ref[...]
    top = jnp.max(s, axis=1, keepdims=True)
    p = jnp.exp(s - top)
    total = jnp.sum(p, axis=1, keepdims=True)
    acc = dot_t(p.astype(jnp.bfloat16), keys[:KV_RANK])
    out_ref[:, :KV_RANK] = (acc / total).astype(jnp.bfloat16)
    lse = jnp.broadcast_to(top + jnp.log(total), (q_ref.shape[0], 128))
    hi = lse.astype(jnp.bfloat16).astype(jnp.float32)
    mid = (lse - hi).astype(jnp.bfloat16).astype(jnp.float32)
    low = lse - hi - mid
    lane = lax.broadcasted_iota(jnp.int32, lse.shape, 1)
    out_ref[:, KV_RANK:] = jnp.where(
        lane == 0, hi, jnp.where(lane == 1, mid, jnp.where(lane == 2, low, 0.0))
    ).astype(jnp.bfloat16)


def decode_attention(q, kv, bias):
    rows, width = q.shape
    return pl.pallas_call(
        dec_attn_kernel,
        out_shape=jax.ShapeDtypeStruct((rows, KV_RANK + 128), jnp.bfloat16),
        compiler_params=pltpu.CompilerParams(vmem_limit_bytes=16 << 20),
        cost_estimate=pl.CostEstimate(
            flops=2 * rows * bias.shape[1] * (width + KV_RANK),
            bytes_accessed=4 * rows * width,
            transcendentals=rows * bias.shape[1],
        ),
        name="decode_attention",
    )(q, *kv, bias)


def combine_kernel(parts_ref, out_ref):
    n, rows, _ = parts_ref.shape
    lses = [
        jnp.sum(parts_ref[i, :, KV_RANK:].astype(jnp.float32), axis=1, keepdims=True)
        for i in range(n)
    ]
    top = functools.reduce(jnp.maximum, lses)
    shares = [jnp.exp(x - top) for x in lses]
    total = functools.reduce(jnp.add, shares)
    acc = sum(shares[i] * parts_ref[i, :, :KV_RANK].astype(jnp.float32) for i in range(n))
    out_ref[...] = (acc / total).astype(jnp.bfloat16)


def project_kernel(lat_ref, w_ref, out_ref):
    heads, _, rank = w_ref.shape
    total = None
    for h in range(heads):
        part = dot_t(lat_ref[:, h * rank : (h + 1) * rank], w_ref[h])
        total = part if total is None else total + part
    out_ref[...] = total.astype(jnp.bfloat16)


def project(latent, w_out):
    rows, depth = latent.shape
    heads, cols, rank = w_out.shape
    return pl.pallas_call(
        project_kernel,
        out_shape=jax.ShapeDtypeStruct((rows, cols), jnp.bfloat16),
        compiler_params=pltpu.CompilerParams(vmem_limit_bytes=20 << 20),
        cost_estimate=pl.CostEstimate(
            flops=2 * rows * depth * cols, bytes_accessed=2 * depth * cols, transcendentals=0
        ),
        name="project",
    )(latent, w_out)


def prefill_kernel(piece, pieces, q_ref, bias_ref, own_hbm, other_hbm, after, *rest):
    own_buf, other_buf, acc_buf, sems, acc_sem = rest[-5:]
    steps, group, _, _ = own_buf.shape
    rows = q_ref.shape[0]

    def copies(i):
        at = pl.ds((piece * steps + i) * group, group)
        return (
            pltpu.make_async_copy(own_hbm.at[at], own_buf.at[i], sems.at[0, i]),
            pltpu.make_async_copy(other_hbm.at[at], other_buf.at[i], sems.at[1, i]),
        )

    for i in range(steps):
        for copy in copies(i):
            copy.start()
    if piece > 0:
        acc_copy = pltpu.make_async_copy(rest[0], acc_buf, acc_sem)
        acc_copy.start()
    q = q_ref[...]
    top = total = acc = None
    for i in range(steps):
        for copy in copies(i):
            copy.wait()
        keys = jnp.concatenate(take(own_buf.at[i], range(group)) + take(other_buf.at[i], range(group)), axis=1)
        s = jnp.dot(q, keys, preferred_element_type=jnp.float32) * SCALE + bias_ref[i]
        best = jnp.max(s, axis=1, keepdims=True)
        new = best if top is None else jnp.maximum(top, best)
        p = jnp.exp(s - new)
        p_sum = jnp.sum(p, axis=1, keepdims=True)
        part = dot_t(p.astype(jnp.bfloat16), keys[:KV_RANK])
        if top is None:
            total, acc = p_sum, part
        else:
            fade = jnp.exp(top - new)
            total, acc = total * fade + p_sum, acc * fade + part
        top = new
    if piece > 0:
        old, old_total = rest[1][:, 0:1], rest[1][:, 1:2]
        new = jnp.maximum(top, old)
        fade, old_fade = jnp.exp(top - new), jnp.exp(old - new)
        acc_copy.wait()
        total = total * fade + old_total * old_fade
        acc = acc * fade + acc_buf[...] * old_fade
        top = new
        rest = rest[2:]
    rest[2][...] = jnp.zeros_like(rest[2])
    if piece == pieces - 1:
        rest[0][...] = (acc / total).astype(jnp.bfloat16)
        rest[1][...] = jnp.zeros_like(rest[1])
    else:
        rest[0][...] = acc
        lane = lax.broadcasted_iota(jnp.int32, rest[1].shape, 1)
        rest[1][...] = jnp.where(lane == 0, top, total)


def prefill(piece, pieces, q, bias, own, other, after, so_far):
    rows, width = q.shape
    blocks, _, half = own.shape
    steps, _, positions = bias.shape
    steps //= pieces
    whole = pl.BlockSpec((rows, KV_RANK), lambda i: (0, 0))
    stats = pl.BlockSpec((rows, 128), lambda i: (0, 0))
    last = piece == pieces - 1
    anywhere = pl.BlockSpec(memory_space=pl.ANY)
    buf = pltpu.VMEM((steps, blocks // pieces // steps, width, half), jnp.bfloat16)
    return pl.pallas_call(
        functools.partial(prefill_kernel, piece, pieces),
        grid=(1,),
        in_specs=[
            pl.BlockSpec((rows, width), lambda i: (0, 0)),
            pl.BlockSpec((steps, 1, positions), lambda i: (piece, 0, 0)),
            anywhere,
            anywhere,
            anywhere,
        ]
        + ([anywhere, stats] if so_far else []),
        out_specs=[whole, stats, pl.BlockSpec(memory_space=pltpu.VMEM)],
        out_shape=[
            jax.ShapeDtypeStruct((rows, KV_RANK), jnp.bfloat16 if last else jnp.float32),
            jax.ShapeDtypeStruct((rows, 128), jnp.float32),
            pltpu.VMEM((8, 128), jnp.float32),
        ],
        scratch_shapes=[
            buf,
            buf,
            pltpu.VMEM((rows, KV_RANK), jnp.float32),
            pltpu.SemaphoreType.DMA((2, steps)),
            pltpu.SemaphoreType.DMA,
        ],
        compiler_params=pltpu.CompilerParams(vmem_limit_bytes=BIG_VMEM),
        cost_estimate=pl.CostEstimate(
            flops=2 * rows * steps * positions * (width + KV_RANK),
            bytes_accessed=2 * steps * positions * width,
            transcendentals=rows * steps * positions,
        ),
        name="prefill",
    )(q, bias, own, other, after, *so_far[:2])


def expert_kernel(
    core_ref, x_ref, gain_ref, gate_hbm, up_hbm, down_hbm, keep_ref, send_ref, gate_buf, up_buf, down_buf, sems, down_sems
):
    halves, _, width = x_ref.shape
    parts, chunk, _ = gate_buf.shape
    core = core_ref[0]

    def copies(i):
        rows = pl.ds(i * chunk, chunk)
        return (
            pltpu.make_async_copy(gate_hbm.at[rows, :], gate_buf.at[i], sems.at[0, i]),
            pltpu.make_async_copy(up_hbm.at[rows, :], up_buf.at[i], sems.at[1, i]),
        )

    def down_copy(i):
        return pltpu.make_async_copy(
            down_hbm.at[:, pl.ds(i * chunk, chunk)], down_buf.at[i], down_sems.at[i]
        )

    def start(i):
        if i < parts:
            for copy in copies(i):
                copy.start()
        elif i < 2 * parts:
            down_copy(i - parts).start()

    for i in range(AHEAD):
        start(i)
    square = 0.0
    for half in range(halves):
        x = x_ref[half].astype(jnp.float32)
        square = square + jnp.sum(x * x, axis=1, keepdims=True)
    scale = lax.rsqrt(square / (halves * width) + 1e-06)
    gate = up = None
    for i in range(parts):
        half, at = divmod(i * chunk, width)
        x = x_ref[half, :, at : at + chunk].astype(jnp.float32) * scale
        x = (x * gain_ref[:, i * chunk : (i + 1) * chunk]).astype(jnp.bfloat16)
        for copy in copies(i):
            copy.wait()
        start(i + AHEAD)
        g = jnp.dot(x, gate_buf[i], preferred_element_type=jnp.float32)
        u = jnp.dot(x, up_buf[i], preferred_element_type=jnp.float32)
        gate = g if gate is None else gate + g
        up = u if up is None else up + u
    inner = (jax.nn.silu(gate) * up).astype(jnp.bfloat16)
    for i in range(parts):
        down_copy(i).wait()
        start(parts + i + AHEAD)
        out = jnp.dot(inner, down_buf[i], preferred_element_type=jnp.float32).astype(jnp.bfloat16)
        half, at = divmod(i * chunk, width)

        @pl.when(core == half)
        def _():
            keep_ref[:, at : at + chunk] = out

        @pl.when(core != half)
        def _():
            send_ref[:, at : at + chunk] = out


def expert(core, x, gain, w_gate, w_up, w_down):
    _, rows, width = x.shape
    depth, hidden = w_gate.shape
    chunk = 896
    parts = depth // chunk
    vmem, anywhere = pl.BlockSpec(memory_space=pltpu.VMEM), pl.BlockSpec(memory_space=pl.ANY)
    return pl.pallas_call(
        expert_kernel,
        in_specs=[pl.BlockSpec(memory_space=pltpu.SMEM), vmem, vmem] + [anywhere] * 3,
        out_specs=[vmem, vmem],
        out_shape=[jax.ShapeDtypeStruct((rows, width), jnp.bfloat16)] * 2,
        scratch_shapes=[
            pltpu.VMEM((parts, chunk, hidden), jnp.bfloat16),
            pltpu.VMEM((parts, chunk, hidden), jnp.bfloat16),
            pltpu.VMEM((parts, hidden, chunk), jnp.bfloat16),
            pltpu.SemaphoreType.DMA((2, parts)),
            pltpu.SemaphoreType.DMA((parts,)),
        ],
        compiler_params=pltpu.CompilerParams(vmem_limit_bytes=EXPERT_VMEM),
        cost_estimate=pl.CostEstimate(
            flops=6 * rows * depth * hidden, bytes_accessed=6 * depth * hidden, transcendentals=rows * hidden
        ),
        name="expert",
    )(core, x, gain, w_gate, w_up, w_down)


def collect_kernel(weight_ref, returned_ref, state_ref, dispatch_ref, *rest):
    out_ref, outgoing_ref = rest[-2:]
    added = jnp.dot(
        weight_ref[...],
        returned_ref[...].astype(jnp.float32),
        precision=lax.Precision.HIGHEST,
        preferred_element_type=jnp.float32,
    )
    state = (state_ref[...].astype(jnp.float32) + added).astype(jnp.bfloat16)
    out_ref[...] = state
    outgoing_ref[...] = jnp.dot(dispatch_ref[...], state, preferred_element_type=jnp.float32).astype(jnp.bfloat16)


def collect_rows(weight, returned, state, dispatch, extra):
    vmem = pl.BlockSpec(memory_space=pltpu.VMEM)
    return pl.pallas_call(
        collect_kernel,
        in_specs=[vmem] * 4 + [pl.BlockSpec(memory_space=pl.ANY)] * len(extra),
        out_specs=[vmem, vmem],
        out_shape=[
            jax.ShapeDtypeStruct(state.shape, state.dtype),
            jax.ShapeDtypeStruct((dispatch.shape[0], state.shape[1]), state.dtype),
        ],
        compiler_params=pltpu.CompilerParams(vmem_limit_bytes=8 << 20),
        name="collect_rows",
    )(weight, returned, state, dispatch, *extra)


def per_device(
    stretch_queries,
    cache_latent,
    doc_lengths,
    decode_queries,
    w_attn_out,
    decode_hidden,
    norm_gain,
    w_gate,
    w_up,
    w_down,
    routes,
    gate_weights,
):
    tokens, heads, width = stretch_queries.shape
    rows, dec_heads, _ = decode_queries.shape
    block = cache_latent.shape[0]
    half = block // 2
    ctx_size = lax.axis_size(CTX)
    model = decode_hidden.shape[1]
    core = lax.axis_index("core")
    x_hi = lax.axis_index("x_hi")
    x_lo = lax.axis_index("x_lo")
    quarter = model // 4
    my_quarter = core * 2 + x_hi

    mine = lax.dynamic_slice_in_dim(cache_latent.T, core * half, half, 1)

    line = jnp.stack([mine] + [shift(mine, "y", by) for by in TURNS[1:]])
    dec_q = decode_queries.reshape(rows * dec_heads, width)
    group_q = spread(dec_q, SHARDS)
    shards = group_q.shape[0]
    plane = jnp.concatenate(
        [line]
        + [
            lax.ppermute(part, X, [(x_index(i), x_index(i + by)) for i in range(4)])
            for part, by in ((line[:2], 1), (line[2:], 3))
        ]
    )
    plane = tie(plane, group_q, vmem=12 << 20)
    plane_other = shift(plane, "core", 1)
    y = lax.axis_index("y")
    z = lax.axis_index("z")
    y_at = (y - jnp.array(TURNS, jnp.int32)) % 4

    def plane_at(z_at):
        return ((x_lo ^ jnp.arange(2, dtype=jnp.int32)[:, None]) * 4 + z_at) * 4 + y_at

    def lengths_of(blocks):
        hit = blocks[..., None] == jnp.arange(doc_lengths.shape[0], dtype=jnp.int32)
        return jnp.sum(jnp.where(hit, doc_lengths, 0), axis=-1)

    line_len = lengths_of(plane_at(z).reshape(8))
    place = jnp.arange(half, dtype=jnp.int32)

    def bias_of(which, lengths):
        usable = place + which * half < lengths[..., None]
        return jnp.where(usable, 0.0, MASKED).astype(jnp.float32)

    line_bias = jnp.stack([bias_of(core, line_len), bias_of(1 - core, line_len)])
    parts = decode_attention(
        group_q.reshape(shards * rows * dec_heads, width),
        (plane, plane_other),
        line_bias.reshape(1, 8 * block),
    )
    parts = lax.all_to_all(
        parts.reshape(shards, rows * dec_heads, KV_RANK + 128), SHARDS, 0, 0, tiled=True
    )
    dec_latent = pl.pallas_call(
        combine_kernel,
        out_shape=jax.ShapeDtypeStruct((rows * dec_heads, KV_RANK), jnp.bfloat16),
        compiler_params=pltpu.CompilerParams(vmem_limit_bytes=8 << 20),
        name="combine_shards",
    )(parts)

    all_latent = spread(dec_latent.reshape(rows, dec_heads * KV_RANK), CTX)
    cols = w_attn_out.shape[2]
    partial_attn = project(
        all_latent.reshape(ctx_size * rows, dec_heads * KV_RANK), jnp.swapaxes(w_attn_out, 1, 2)
    )
    both = lax.all_gather(partial_attn, "core", axis=0)
    attn_cols = jnp.sum(both.astype(jnp.float32), axis=0).astype(jnp.bfloat16)
    attn_cols = jnp.broadcast_to(
        attn_cols.reshape(ctx_size, 1, rows, cols), (ctx_size, 2, rows, cols)
    ).reshape(ctx_size * 2, rows, cols)
    attn_parts = lax.all_to_all(attn_cols, LANE, 0, 0, tiled=True)
    attn_parts = attn_parts.reshape(4, ctx_size // 4, 2, rows, cols)
    attn_parts = lax.dynamic_index_in_dim(attn_parts, my_quarter, 0, keepdims=False)
    attn_out = jnp.sum(attn_parts.astype(jnp.float32), axis=1).astype(jnp.bfloat16)
    attn_out = jnp.swapaxes(attn_out.reshape(8, rows, cols), 0, 1).reshape(rows, quarter)
    hidden_quarter = lax.dynamic_slice_in_dim(decode_hidden, my_quarter * quarter, quarter, 1)
    state = (hidden_quarter.astype(jnp.float32) + attn_out.astype(jnp.float32)).astype(jnp.bfloat16)

    experts = jnp.arange(ctx_size, dtype=jnp.int32)
    hits = routes[..., None] == experts
    used = jnp.any(hits, axis=2)
    weight = jnp.sum(jnp.where(hits, gate_weights[..., None], 0.0), axis=2)
    counted = used.astype(jnp.int32)
    earlier = jnp.cumsum(counted, axis=1) - counted
    placed = used[..., None] & (earlier[..., None] == jnp.arange(SLOTS, dtype=jnp.int32))
    dispatch = jnp.moveaxis(placed, 1, -1).astype(jnp.bfloat16)
    dispatch = jnp.broadcast_to(dispatch[:, :, None], (STEPS, ctx_size, 2, SLOTS, rows))
    dispatch = dispatch.reshape(STEPS, ctx_size * 2 * SLOTS, rows)
    collect = jnp.where(placed, weight[..., None], 0.0)
    collect = jnp.broadcast_to(collect[:, :, :, None, :], (STEPS, rows, ctx_size, 2, SLOTS))
    collect = collect.reshape(STEPS, rows, ctx_size * 2 * SLOTS)

    core_arr = core.astype(jnp.int32).reshape(1)
    gain = norm_gain.reshape(1, model)

    gathered = lax.all_gather(tie(plane, all_latent), "z", axis=0, tiled=True)
    all_len = lengths_of(plane_at(jnp.arange(4, dtype=jnp.int32)[:, None, None]).reshape(8, 4))
    bias = jnp.stack([bias_of(core, all_len), bias_of(1 - core, all_len)], axis=1)
    bias = bias.reshape(8, 1, KV_ARRAYS * 4 * half)
    flat_q = stretch_queries.reshape(tokens * heads, width)
    sums = ()

    outgoing = jnp.dot(dispatch[0], state, preferred_element_type=jnp.float32).astype(jnp.bfloat16)
    for step in range(STEPS):
        outgoing = outgoing.reshape(ctx_size * 2, SLOTS, quarter)
        received = lax.all_to_all(outgoing, LANE, 0, 0, tiled=True)
        if step > 0:
            sums = prefill(2 * step - 2, PIECES, flat_q, bias, *kv, outgoing, sums)
            received = tie(received, sums[2], vmem=4 << 20)
        received = received.reshape(ctx_size, 2, SLOTS, quarter)
        received = jnp.swapaxes(received, 1, 2).reshape(ctx_size * SLOTS, 2 * quarter)
        received = lax.all_gather(received, "core", axis=0)
        keep, send = expert(core_arr, received, gain, w_gate[0], w_up[0], w_down[0])
        partial_out = (keep.astype(jnp.float32) + shift(send, "core", 1).astype(jnp.float32)).astype(jnp.bfloat16)
        if step == 0:
            gathered = tie(gathered, partial_out)
            kv = [gathered, shift(gathered, "core", 1)]
        extra = []
        if step > 0:
            sums = prefill(2 * step - 1, PIECES, flat_q, bias, *kv, partial_out, sums)
            extra = [sums[2]]
        partial_out = partial_out.reshape(ctx_size, SLOTS, 2, quarter)
        partial_out = jnp.swapaxes(partial_out, 1, 2).reshape(ctx_size * 2, SLOTS, quarter)
        returned = lax.all_to_all(partial_out, LANE, 0, 0, tiled=True)
        returned = returned.reshape(ctx_size * 2 * SLOTS, quarter)
        state, outgoing = collect_rows(
            collect[step], returned, state, dispatch[min(step + 1, STEPS - 1)], extra
        )
    decode_out = lax.all_gather(state, HEAD, axis=0)
    decode_out = decode_out.reshape(2, 2, rows, quarter).transpose(2, 1, 0, 3).reshape(rows, model)
    return sums[0].reshape(tokens, heads, KV_RANK), decode_out


def solution(mesh):
    names = [name for axis in mesh.axis_names for name, _ in SPLIT[axis]]
    sizes = [size for axis in mesh.axis_names for _, size in SPLIT[axis]]
    fine = Mesh(mesh.devices.reshape(sizes), names)
    return jax.shard_map(
        per_device,
        mesh=fine,
        in_specs=(
            P(CTX, HEAD, None),
            P(CTX, None),
            P(),
            P(CTX, HEAD, None),
            P(HEAD, None, CTX),
            P(CTX, None),
            P(),
            P(CTX, None, HEAD),
            P(CTX, None, HEAD),
            P(CTX, HEAD, None),
            P(None, CTX, None),
            P(None, CTX, None),
        ),
        out_specs=(P(CTX, HEAD, None), P(CTX, None)),
        check_vma=False,
    )
```

```python
import functools

import jax
import jax.numpy as jnp
from jax import lax
from jax.experimental import pallas as pl
from jax.experimental.pallas import tpu as pltpu
from jax.sharding import Mesh, PartitionSpec as P

KV_RANK = 512
STEPS = 3
SLOTS = 2
SCALE = 0.07216878364870322
MASKED = -1e30
KV_ARRAYS = 2
PIECES = 2 * STEPS - 2
TURNS = (0, 1, 3, 2)
BIG_VMEM = 56 << 20
EXPERT_VMEM = 50 << 20
AHEAD = 8

SPLIT = {"ctx": (("x_lo", 2), ("z", 4), ("y", 4)), "head": (("x_hi", 2), ("core", 2))}
CTX = ("x_lo", "z", "y")
HEAD = ("x_hi", "core")
SHARDS = "z"
LANE = CTX + ("x_hi",)
X = ("x_lo", "x_hi")


def shift(x, axis, by):
    n = lax.axis_size(axis)
    return lax.ppermute(x, axis, [(i, (i + by) % n) for i in range(n)])


def x_index(x):
    return x % 2 * 2 + x % 4 // 2


def spread(x, axes):
    n = lax.axis_size(axes)
    return lax.all_to_all(jnp.broadcast_to(x[None], (n,) + x.shape), axes, 0, 0, tiled=True)


def dot_t(a, b):
    return lax.dot_general(a, b, (((1,), (1,)), ((), ())), preferred_element_type=jnp.float32)


def tie(x, *after, vmem=None):
    anywhere = pl.BlockSpec(memory_space=pl.ANY)
    return pl.pallas_call(
        lambda *refs: None,
        in_specs=[anywhere] * (1 + len(after)),
        out_specs=anywhere,
        out_shape=jax.ShapeDtypeStruct(x.shape, x.dtype),
        input_output_aliases={0: 0},
        compiler_params=pltpu.CompilerParams(vmem_limit_bytes=vmem or BIG_VMEM),
        cost_estimate=pl.CostEstimate(flops=0, bytes_accessed=0, transcendentals=0),
        name="tie",
    )(x, *after)


def take(ref, at):
    return [ref[i] for i in at]


def dec_attn_kernel(q_ref, *rest):
    bias_ref, out_ref = rest[-2:]
    keys = jnp.concatenate([block for ref in rest[:-2] for block in take(ref, range(ref.shape[0]))], axis=1)
    s = jnp.dot(q_ref[...], keys, preferred_element_type=jnp.float32) * SCALE + bias_ref[...]
    top = jnp.max(s, axis=1, keepdims=True)
    p = jnp.exp(s - top)
    total = jnp.sum(p, axis=1, keepdims=True)
    acc = dot_t(p.astype(jnp.bfloat16), keys[:KV_RANK])
    out_ref[:, :KV_RANK] = (acc / total).astype(jnp.bfloat16)
    lse = jnp.broadcast_to(top + jnp.log(total), (q_ref.shape[0], 128))
    hi = lse.astype(jnp.bfloat16).astype(jnp.float32)
    mid = (lse - hi).astype(jnp.bfloat16).astype(jnp.float32)
    low = lse - hi - mid
    lane = lax.broadcasted_iota(jnp.int32, lse.shape, 1)
    out_ref[:, KV_RANK:] = jnp.where(
        lane == 0, hi, jnp.where(lane == 1, mid, jnp.where(lane == 2, low, 0.0))
    ).astype(jnp.bfloat16)


def decode_attention(q, kv, bias):
    rows, width = q.shape
    return pl.pallas_call(
        dec_attn_kernel,
        out_shape=jax.ShapeDtypeStruct((rows, KV_RANK + 128), jnp.bfloat16),
        compiler_params=pltpu.CompilerParams(vmem_limit_bytes=16 << 20),
        cost_estimate=pl.CostEstimate(
            flops=2 * rows * bias.shape[1] * (width + KV_RANK),
            bytes_accessed=4 * rows * width,
            transcendentals=rows * bias.shape[1],
        ),
        name="decode_attention",
    )(q, *kv, bias)


def combine_kernel(parts_ref, out_ref):
    n, rows, _ = parts_ref.shape
    lses = [
        jnp.sum(parts_ref[i, :, KV_RANK:].astype(jnp.float32), axis=1, keepdims=True)
        for i in range(n)
    ]
    top = functools.reduce(jnp.maximum, lses)
    shares = [jnp.exp(x - top) for x in lses]
    total = functools.reduce(jnp.add, shares)
    acc = sum(shares[i] * parts_ref[i, :, :KV_RANK].astype(jnp.float32) for i in range(n))
    out_ref[...] = (acc / total).astype(jnp.bfloat16)


def project_kernel(lat_ref, w_ref, out_ref):
    heads, _, rank = w_ref.shape
    total = None
    for h in range(heads):
        part = dot_t(lat_ref[:, h * rank : (h + 1) * rank], w_ref[h])
        total = part if total is None else total + part
    out_ref[...] = total.astype(jnp.bfloat16)


def project(latent, w_out):
    rows, depth = latent.shape
    heads, cols, rank = w_out.shape
    return pl.pallas_call(
        project_kernel,
        out_shape=jax.ShapeDtypeStruct((rows, cols), jnp.bfloat16),
        compiler_params=pltpu.CompilerParams(vmem_limit_bytes=20 << 20),
        cost_estimate=pl.CostEstimate(
            flops=2 * rows * depth * cols, bytes_accessed=2 * depth * cols, transcendentals=0
        ),
        name="project",
    )(latent, w_out)


def prefill_kernel(piece, pieces, q_ref, bias_ref, own_hbm, other_hbm, after, *rest):
    own_buf, other_buf, acc_buf, sems, acc_sem = rest[-5:]
    steps, group, _, _ = own_buf.shape
    rows = q_ref.shape[0]

    def copies(i):
        at = pl.ds((piece * steps + i) * group, group)
        return (
            pltpu.make_async_copy(own_hbm.at[at], own_buf.at[i], sems.at[0, i]),
            pltpu.make_async_copy(other_hbm.at[at], other_buf.at[i], sems.at[1, i]),
        )

    for i in range(steps):
        for copy in copies(i):
            copy.start()
    if piece > 0:
        acc_copy = pltpu.make_async_copy(rest[0], acc_buf, acc_sem)
        acc_copy.start()
    q = q_ref[...]
    top = total = acc = None
    for i in range(steps):
        for copy in copies(i):
            copy.wait()
        keys = jnp.concatenate(take(own_buf.at[i], range(group)) + take(other_buf.at[i], range(group)), axis=1)
        s = jnp.dot(q, keys, preferred_element_type=jnp.float32) * SCALE + bias_ref[i]
        best = jnp.max(s, axis=1, keepdims=True)
        new = best if top is None else jnp.maximum(top, best)
        p = jnp.exp(s - new)
        p_sum = jnp.sum(p, axis=1, keepdims=True)
        part = dot_t(p.astype(jnp.bfloat16), keys[:KV_RANK])
        if top is None:
            total, acc = p_sum, part
        else:
            fade = jnp.exp(top - new)
            total, acc = total * fade + p_sum, acc * fade + part
        top = new
    if piece > 0:
        old, old_total = rest[1][:, 0:1], rest[1][:, 1:2]
        new = jnp.maximum(top, old)
        fade, old_fade = jnp.exp(top - new), jnp.exp(old - new)
        acc_copy.wait()
        total = total * fade + old_total * old_fade
        acc = acc * fade + acc_buf[...] * old_fade
        top = new
        rest = rest[2:]
    rest[2][...] = jnp.zeros_like(rest[2])
    if piece == pieces - 1:
        rest[0][...] = (acc / total).astype(jnp.bfloat16)
        rest[1][...] = jnp.zeros_like(rest[1])
    else:
        rest[0][...] = acc
        lane = lax.broadcasted_iota(jnp.int32, rest[1].shape, 1)
        rest[1][...] = jnp.where(lane == 0, top, total)


def prefill(piece, pieces, q, bias, own, other, after, so_far):
    rows, width = q.shape
    blocks, _, half = own.shape
    steps, _, positions = bias.shape
    steps //= pieces
    whole = pl.BlockSpec((rows, KV_RANK), lambda i: (0, 0))
    stats = pl.BlockSpec((rows, 128), lambda i: (0, 0))
    last = piece == pieces - 1
    anywhere = pl.BlockSpec(memory_space=pl.ANY)
    buf = pltpu.VMEM((steps, blocks // pieces // steps, width, half), jnp.bfloat16)
    return pl.pallas_call(
        functools.partial(prefill_kernel, piece, pieces),
        grid=(1,),
        in_specs=[
            pl.BlockSpec((rows, width), lambda i: (0, 0)),
            pl.BlockSpec((steps, 1, positions), lambda i: (piece, 0, 0)),
            anywhere,
            anywhere,
            anywhere,
        ]
        + ([anywhere, stats] if so_far else []),
        out_specs=[whole, stats, pl.BlockSpec(memory_space=pltpu.VMEM)],
        out_shape=[
            jax.ShapeDtypeStruct((rows, KV_RANK), jnp.bfloat16 if last else jnp.float32),
            jax.ShapeDtypeStruct((rows, 128), jnp.float32),
            pltpu.VMEM((8, 128), jnp.float32),
        ],
        scratch_shapes=[
            buf,
            buf,
            pltpu.VMEM((rows, KV_RANK), jnp.float32),
            pltpu.SemaphoreType.DMA((2, steps)),
            pltpu.SemaphoreType.DMA,
        ],
        compiler_params=pltpu.CompilerParams(vmem_limit_bytes=BIG_VMEM),
        cost_estimate=pl.CostEstimate(
            flops=2 * rows * steps * positions * (width + KV_RANK),
            bytes_accessed=2 * steps * positions * width,
            transcendentals=rows * steps * positions,
        ),
        name="prefill",
    )(q, bias, own, other, after, *so_far[:2])


def expert_kernel(
    core_ref, x_ref, gain_ref, gate_hbm, up_hbm, down_hbm, keep_ref, send_ref, gate_buf, up_buf, down_buf, sems, down_sems
):
    halves, _, width = x_ref.shape
    parts, chunk, _ = gate_buf.shape
    core = core_ref[0]

    def copies(i):
        rows = pl.ds(i * chunk, chunk)
        return (
            pltpu.make_async_copy(gate_hbm.at[rows, :], gate_buf.at[i], sems.at[0, i]),
            pltpu.make_async_copy(up_hbm.at[rows, :], up_buf.at[i], sems.at[1, i]),
        )

    def down_copy(i):
        return pltpu.make_async_copy(
            down_hbm.at[:, pl.ds(i * chunk, chunk)], down_buf.at[i], down_sems.at[i]
        )

    def start(i):
        if i < parts:
            for copy in copies(i):
                copy.start()
        else:
            for j in range(2 * (i - parts), min(2 * (i - parts) + 2, parts)):
                down_copy(j).start()

    for i in range(AHEAD):
        start(i)
    square = 0.0
    for half in range(halves):
        x = x_ref[half].astype(jnp.float32)
        square = square + jnp.sum(x * x, axis=1, keepdims=True)
    scale = lax.rsqrt(square / (halves * width) + 1e-06)
    gate = up = None
    for i in range(parts):
        half, at = divmod(i * chunk, width)
        x = x_ref[half, :, at : at + chunk].astype(jnp.float32) * scale
        x = (x * gain_ref[:, i * chunk : (i + 1) * chunk]).astype(jnp.bfloat16)
        for copy in copies(i):
            copy.wait()
        start(i + AHEAD)
        g = jnp.dot(x, gate_buf[i], preferred_element_type=jnp.float32)
        u = jnp.dot(x, up_buf[i], preferred_element_type=jnp.float32)
        gate = g if gate is None else gate + g
        up = u if up is None else up + u
    inner = (jax.nn.silu(gate) * up).astype(jnp.bfloat16)
    for i in range(parts):
        down_copy(i).wait()
        if i % 2 == 1:
            start(parts + i // 2 + AHEAD)
        out = jnp.dot(inner, down_buf[i], preferred_element_type=jnp.float32).astype(jnp.bfloat16)
        half, at = divmod(i * chunk, width)

        @pl.when(core == half)
        def _():
            keep_ref[:, at : at + chunk] = out

        @pl.when(core != half)
        def _():
            send_ref[:, at : at + chunk] = out


def expert(core, x, gain, w_gate, w_up, w_down):
    _, rows, width = x.shape
    depth, hidden = w_gate.shape
    chunk = 896
    parts = depth // chunk
    vmem, anywhere = pl.BlockSpec(memory_space=pltpu.VMEM), pl.BlockSpec(memory_space=pl.ANY)
    return pl.pallas_call(
        expert_kernel,
        in_specs=[pl.BlockSpec(memory_space=pltpu.SMEM), vmem, vmem] + [anywhere] * 3,
        out_specs=[vmem, vmem],
        out_shape=[jax.ShapeDtypeStruct((rows, width), jnp.bfloat16)] * 2,
        scratch_shapes=[
            pltpu.VMEM((parts, chunk, hidden), jnp.bfloat16),
            pltpu.VMEM((parts, chunk, hidden), jnp.bfloat16),
            pltpu.VMEM((parts, hidden, chunk), jnp.bfloat16),
            pltpu.SemaphoreType.DMA((2, parts)),
            pltpu.SemaphoreType.DMA((parts,)),
        ],
        compiler_params=pltpu.CompilerParams(vmem_limit_bytes=EXPERT_VMEM),
        cost_estimate=pl.CostEstimate(
            flops=6 * rows * depth * hidden, bytes_accessed=6 * depth * hidden, transcendentals=rows * hidden
        ),
        name="expert",
    )(core, x, gain, w_gate, w_up, w_down)


def collect_kernel(weight_ref, returned_ref, state_ref, dispatch_ref, *rest):
    added = jnp.dot(
        weight_ref[...],
        returned_ref[...].astype(jnp.float32),
        precision=lax.Precision.HIGHEST,
        preferred_element_type=jnp.float32,
    )
    state = (state_ref[...].astype(jnp.float32) + added).astype(jnp.bfloat16)
    rest[-2][...] = state
    rest[-1][...] = jnp.dot(dispatch_ref[...], state, preferred_element_type=jnp.float32).astype(jnp.bfloat16)


def collect_rows(weight, returned, state, dispatch, extra):
    vmem = pl.BlockSpec(memory_space=pltpu.VMEM)
    return pl.pallas_call(
        collect_kernel,
        in_specs=[vmem] * 4 + [pl.BlockSpec(memory_space=pl.ANY)] * len(extra),
        out_specs=[vmem, vmem],
        out_shape=[
            jax.ShapeDtypeStruct(state.shape, state.dtype),
            jax.ShapeDtypeStruct((dispatch.shape[0], state.shape[1]), state.dtype),
        ],
        compiler_params=pltpu.CompilerParams(vmem_limit_bytes=8 << 20),
        name="collect_rows",
    )(weight, returned, state, dispatch, *extra)


def per_device(
    stretch_queries,
    cache_latent,
    doc_lengths,
    decode_queries,
    w_attn_out,
    decode_hidden,
    norm_gain,
    w_gate,
    w_up,
    w_down,
    routes,
    gate_weights,
):
    tokens, heads, width = stretch_queries.shape
    rows, dec_heads, _ = decode_queries.shape
    block = cache_latent.shape[0]
    half = block // 2
    ctx_size = lax.axis_size(CTX)
    model = decode_hidden.shape[1]
    core = lax.axis_index("core")
    x_hi = lax.axis_index("x_hi")
    x_lo = lax.axis_index("x_lo")
    quarter = model // 4
    my_quarter = core * 2 + x_hi

    mine = lax.dynamic_slice_in_dim(cache_latent.T, core * half, half, 1)

    line = jnp.stack([mine] + [shift(mine, "y", by) for by in TURNS[1:]])
    dec_q = decode_queries.reshape(rows * dec_heads, width)
    group_q = spread(dec_q, SHARDS)
    shards = group_q.shape[0]
    plane = jnp.concatenate(
        [line]
        + [
            lax.ppermute(part, X, [(x_index(i), x_index(i + by)) for i in range(4)])
            for part, by in ((line[:2], 1), (line[2:], 3))
        ]
    )
    plane = tie(plane, group_q, vmem=12 << 20)
    plane_other = shift(plane, "core", 1)
    y = lax.axis_index("y")
    z = lax.axis_index("z")
    y_at = (y - jnp.array(TURNS, jnp.int32)) % 4

    def plane_at(z_at):
        return ((x_lo ^ jnp.arange(2, dtype=jnp.int32)[:, None]) * 4 + z_at) * 4 + y_at

    def lengths_of(blocks):
        hit = blocks[..., None] == jnp.arange(doc_lengths.shape[0], dtype=jnp.int32)
        return jnp.sum(jnp.where(hit, doc_lengths, 0), axis=-1)

    line_len = lengths_of(plane_at(z).reshape(8))
    place = jnp.arange(half, dtype=jnp.int32)

    def bias_of(which, lengths):
        usable = place + which * half < lengths[..., None]
        return jnp.where(usable, 0.0, MASKED).astype(jnp.float32)

    line_bias = jnp.stack([bias_of(core, line_len), bias_of(1 - core, line_len)])
    parts = decode_attention(
        group_q.reshape(shards * rows * dec_heads, width),
        (plane, plane_other),
        line_bias.reshape(1, 8 * block),
    )
    parts = lax.all_to_all(
        parts.reshape(shards, rows * dec_heads, KV_RANK + 128), SHARDS, 0, 0, tiled=True
    )
    dec_latent = pl.pallas_call(
        combine_kernel,
        out_shape=jax.ShapeDtypeStruct((rows * dec_heads, KV_RANK), jnp.bfloat16),
        compiler_params=pltpu.CompilerParams(vmem_limit_bytes=8 << 20),
        name="combine_shards",
    )(parts)

    all_latent = spread(dec_latent.reshape(rows, dec_heads * KV_RANK), CTX)
    cols = w_attn_out.shape[2]
    partial_attn = project(
        all_latent.reshape(ctx_size * rows, dec_heads * KV_RANK), jnp.swapaxes(w_attn_out, 1, 2)
    )
    both = lax.all_gather(partial_attn, "core", axis=0)
    attn_cols = jnp.sum(both.astype(jnp.float32), axis=0).astype(jnp.bfloat16)
    attn_cols = jnp.broadcast_to(
        attn_cols.reshape(ctx_size, 1, rows, cols), (ctx_size, 2, rows, cols)
    ).reshape(ctx_size * 2, rows, cols)
    attn_parts = lax.all_to_all(attn_cols, LANE, 0, 0, tiled=True)
    attn_parts = attn_parts.reshape(4, ctx_size // 4, 2, rows, cols)
    attn_parts = lax.dynamic_index_in_dim(attn_parts, my_quarter, 0, keepdims=False)
    attn_out = jnp.sum(attn_parts.astype(jnp.float32), axis=1).astype(jnp.bfloat16)
    attn_out = jnp.swapaxes(attn_out.reshape(8, rows, cols), 0, 1).reshape(rows, quarter)
    hidden_quarter = lax.dynamic_slice_in_dim(decode_hidden, my_quarter * quarter, quarter, 1)
    state = (hidden_quarter.astype(jnp.float32) + attn_out.astype(jnp.float32)).astype(jnp.bfloat16)

    experts = jnp.arange(ctx_size, dtype=jnp.int32)
    hits = routes[..., None] == experts
    used = jnp.any(hits, axis=2)
    weight = jnp.sum(jnp.where(hits, gate_weights[..., None], 0.0), axis=2)
    counted = used.astype(jnp.int32)
    earlier = jnp.cumsum(counted, axis=1) - counted
    placed = used[..., None] & (earlier[..., None] == jnp.arange(SLOTS, dtype=jnp.int32))
    dispatch = jnp.moveaxis(placed, 1, -1).astype(jnp.bfloat16)
    dispatch = jnp.broadcast_to(dispatch[:, :, None], (STEPS, ctx_size, 2, SLOTS, rows))
    dispatch = dispatch.reshape(STEPS, ctx_size * 2 * SLOTS, rows)
    collect = jnp.where(placed, weight[..., None], 0.0)
    collect = jnp.broadcast_to(collect[:, :, :, None, :], (STEPS, rows, ctx_size, 2, SLOTS))
    collect = collect.reshape(STEPS, rows, ctx_size * 2 * SLOTS)

    core_arr = core.astype(jnp.int32).reshape(1)
    gain = norm_gain.reshape(1, model)

    gathered = lax.all_gather(tie(plane, all_latent), "z", axis=0, tiled=True)
    all_len = lengths_of(plane_at(jnp.arange(4, dtype=jnp.int32)[:, None, None]).reshape(8, 4))
    bias = jnp.stack([bias_of(core, all_len), bias_of(1 - core, all_len)], axis=1)
    bias = bias.reshape(8, 1, KV_ARRAYS * 4 * half)
    flat_q = stretch_queries.reshape(tokens * heads, width)
    sums = ()

    outgoing = jnp.dot(dispatch[0], state, preferred_element_type=jnp.float32).astype(jnp.bfloat16)
    for step in range(STEPS):
        outgoing = outgoing.reshape(ctx_size * 2, SLOTS, quarter)
        received = lax.all_to_all(outgoing, LANE, 0, 0, tiled=True)
        if step > 0:
            sums = prefill(2 * step - 2, PIECES, flat_q, bias, *kv, outgoing, sums)
            received = tie(received, sums[2], vmem=4 << 20)
        received = received.reshape(ctx_size, 2, SLOTS, quarter)
        received = jnp.swapaxes(received, 1, 2).reshape(ctx_size * SLOTS, 2 * quarter)
        received = lax.all_gather(received, "core", axis=0)
        keep, send = expert(core_arr, received, gain, w_gate[0], w_up[0], w_down[0])
        partial_out = (keep.astype(jnp.float32) + shift(send, "core", 1).astype(jnp.float32)).astype(jnp.bfloat16)
        partial_out = partial_out.reshape(ctx_size, SLOTS, 2, quarter)
        partial_out = jnp.swapaxes(partial_out, 1, 2).reshape(ctx_size * 2, SLOTS, quarter)
        if step == 0:
            gathered = tie(gathered, partial_out)
            kv = [gathered, shift(gathered, "core", 1)]
        extra = []
        if step > 0:
            sums = prefill(2 * step - 1, PIECES, flat_q, bias, *kv, partial_out, sums)
            extra = [sums[2]]
        returned = lax.all_to_all(partial_out, LANE, 0, 0, tiled=True)
        returned = returned.reshape(ctx_size * 2 * SLOTS, quarter)
        state, outgoing = collect_rows(
            collect[step], returned, state, dispatch[min(step + 1, STEPS - 1)], extra
        )
    decode_out = lax.all_gather(state, HEAD, axis=0)
    decode_out = decode_out.reshape(2, 2, rows, quarter).transpose(2, 1, 0, 3).reshape(rows, model)
    return sums[0].reshape(tokens, heads, KV_RANK), decode_out


def solution(mesh):
    names = [name for axis in mesh.axis_names for name, _ in SPLIT[axis]]
    sizes = [size for axis in mesh.axis_names for _, size in SPLIT[axis]]
    fine = Mesh(mesh.devices.reshape(sizes), names)
    return jax.shard_map(
        per_device,
        mesh=fine,
        in_specs=(
            P(CTX, HEAD, None),
            P(CTX, None),
            P(),
            P(CTX, HEAD, None),
            P(HEAD, None, CTX),
            P(CTX, None),
            P(),
            P(CTX, None, HEAD),
            P(CTX, None, HEAD),
            P(CTX, HEAD, None),
            P(None, CTX, None),
            P(None, CTX, None),
        ),
        out_specs=(P(CTX, HEAD, None), P(CTX, None)),
        check_vma=False,
    )
```

```python
import functools

import jax
import jax.numpy as jnp
from jax import lax
from jax.experimental import pallas as pl
from jax.experimental.pallas import tpu as pltpu
from jax.sharding import Mesh, PartitionSpec as P

KV_RANK = 512
STEPS = 3
SLOTS = 2
SCALE = 0.07216878364870322
MASKED = -1e30
KV_ARRAYS = 2
PIECES = 2 * STEPS - 2
TURNS = (0, 1, 3, 2)
BIG_VMEM = 56 << 20
EXPERT_VMEM = 50 << 20
AHEAD = 8

SPLIT = {"ctx": (("x_lo", 2), ("z", 4), ("y", 4)), "head": (("x_hi", 2), ("core", 2))}
CTX = ("x_lo", "z", "y")
HEAD = ("x_hi", "core")
SHARDS = "z"
LANE = CTX + ("x_hi",)
X = ("x_lo", "x_hi")


def shift(x, axis, by):
    n = lax.axis_size(axis)
    return lax.ppermute(x, axis, [(i, (i + by) % n) for i in range(n)])


def x_index(x):
    return x % 2 * 2 + x % 4 // 2


def spread(x, axes):
    n = lax.axis_size(axes)
    return lax.all_to_all(jnp.broadcast_to(x[None], (n,) + x.shape), axes, 0, 0, tiled=True)


def dot_t(a, b):
    return lax.dot_general(a, b, (((1,), (1,)), ((), ())), preferred_element_type=jnp.float32)


def tie(x, *after, vmem=None):
    anywhere = pl.BlockSpec(memory_space=pl.ANY)
    return pl.pallas_call(
        lambda *refs: None,
        in_specs=[anywhere] * (1 + len(after)),
        out_specs=anywhere,
        out_shape=jax.ShapeDtypeStruct(x.shape, x.dtype),
        input_output_aliases={0: 0},
        compiler_params=pltpu.CompilerParams(vmem_limit_bytes=vmem or BIG_VMEM),
        cost_estimate=pl.CostEstimate(flops=0, bytes_accessed=0, transcendentals=0),
        name="tie",
    )(x, *after)


def take(ref, at):
    return [ref[i] for i in at]


def dec_attn_kernel(q_ref, *rest):
    bias_ref, out_ref = rest[-2:]
    keys = jnp.concatenate([block for ref in rest[:-2] for block in take(ref, range(ref.shape[0]))], axis=1)
    s = jnp.dot(q_ref[...], keys, preferred_element_type=jnp.float32) * SCALE + bias_ref[...]
    top = jnp.max(s, axis=1, keepdims=True)
    p = jnp.exp(s - top)
    total = jnp.sum(p, axis=1, keepdims=True)
    acc = dot_t(p.astype(jnp.bfloat16), keys[:KV_RANK])
    out_ref[:, :KV_RANK] = (acc / total).astype(jnp.bfloat16)
    lse = jnp.broadcast_to(top + jnp.log(total), (q_ref.shape[0], 128))
    hi = lse.astype(jnp.bfloat16).astype(jnp.float32)
    mid = (lse - hi).astype(jnp.bfloat16).astype(jnp.float32)
    low = lse - hi - mid
    lane = lax.broadcasted_iota(jnp.int32, lse.shape, 1)
    out_ref[:, KV_RANK:] = jnp.where(
        lane == 0, hi, jnp.where(lane == 1, mid, jnp.where(lane == 2, low, 0.0))
    ).astype(jnp.bfloat16)


def decode_attention(q, kv, bias):
    rows, width = q.shape
    return pl.pallas_call(
        dec_attn_kernel,
        out_shape=jax.ShapeDtypeStruct((rows, KV_RANK + 128), jnp.bfloat16),
        compiler_params=pltpu.CompilerParams(vmem_limit_bytes=16 << 20),
        cost_estimate=pl.CostEstimate(
            flops=2 * rows * bias.shape[1] * (width + KV_RANK),
            bytes_accessed=4 * rows * width,
            transcendentals=rows * bias.shape[1],
        ),
        name="decode_attention",
    )(q, *kv, bias)


def combine_kernel(parts_ref, out_ref):
    n, rows, _ = parts_ref.shape
    lses = [
        jnp.sum(parts_ref[i, :, KV_RANK:].astype(jnp.float32), axis=1, keepdims=True)
        for i in range(n)
    ]
    top = functools.reduce(jnp.maximum, lses)
    shares = [jnp.exp(x - top) for x in lses]
    total = functools.reduce(jnp.add, shares)
    acc = sum(shares[i] * parts_ref[i, :, :KV_RANK].astype(jnp.float32) for i in range(n))
    out_ref[...] = (acc / total).astype(jnp.bfloat16)


def project_kernel(lat_ref, w_ref, out_ref):
    heads, _, rank = w_ref.shape
    total = None
    for h in range(heads):
        lat = lat_ref[:, :, h * rank : (h + 1) * rank].reshape(out_ref.shape[0], rank)
        part = dot_t(lat, w_ref[h])
        total = part if total is None else total + part
    out_ref[...] = total.astype(jnp.bfloat16)


def project(latent, w_out):
    senders, own_rows, depth = latent.shape
    rows = senders * own_rows
    heads, cols, rank = w_out.shape
    return pl.pallas_call(
        project_kernel,
        out_shape=jax.ShapeDtypeStruct((rows, cols), jnp.bfloat16),
        compiler_params=pltpu.CompilerParams(vmem_limit_bytes=20 << 20),
        cost_estimate=pl.CostEstimate(
            flops=2 * rows * depth * cols, bytes_accessed=2 * depth * cols, transcendentals=0
        ),
        name="project",
    )(latent, w_out)


def prefill_kernel(piece, pieces, q_ref, bias_ref, own_hbm, other_hbm, after, *rest):
    own_buf, other_buf, acc_buf, sems, acc_sem = rest[-5:]
    steps, group, _, _ = own_buf.shape
    rows = q_ref.shape[0]

    def copies(i):
        at = pl.ds((piece * steps + i) * group, group)
        return (
            pltpu.make_async_copy(own_hbm.at[at], own_buf.at[i], sems.at[0, i]),
            pltpu.make_async_copy(other_hbm.at[at], other_buf.at[i], sems.at[1, i]),
        )

    for i in range(steps):
        for copy in copies(i):
            copy.start()
    if piece > 0:
        acc_copy = pltpu.make_async_copy(rest[0], acc_buf, acc_sem)
        acc_copy.start()
    q = q_ref[...]
    top = total = acc = None
    for i in range(steps):
        for copy in copies(i):
            copy.wait()
        keys = jnp.concatenate(take(own_buf.at[i], range(group)) + take(other_buf.at[i], range(group)), axis=1)
        s = jnp.dot(q, keys, preferred_element_type=jnp.float32) * SCALE + bias_ref[i]
        best = jnp.max(s, axis=1, keepdims=True)
        new = best if top is None else jnp.maximum(top, best)
        p = jnp.exp(s - new)
        p_sum = jnp.sum(p, axis=1, keepdims=True)
        part = dot_t(p.astype(jnp.bfloat16), keys[:KV_RANK])
        if top is None:
            total, acc = p_sum, part
        else:
            fade = jnp.exp(top - new)
            total, acc = total * fade + p_sum, acc * fade + part
        top = new
    if piece > 0:
        old, old_total = rest[1][:, 0:1], rest[1][:, 1:2]
        new = jnp.maximum(top, old)
        fade, old_fade = jnp.exp(top - new), jnp.exp(old - new)
        acc_copy.wait()
        total = total * fade + old_total * old_fade
        acc = acc * fade + acc_buf[...] * old_fade
        top = new
        rest = rest[2:]
    rest[2][...] = jnp.zeros_like(rest[2])
    if piece == pieces - 1:
        rest[0][...] = (acc / total).astype(jnp.bfloat16)
        rest[1][...] = jnp.zeros_like(rest[1])
    else:
        rest[0][...] = acc
        lane = lax.broadcasted_iota(jnp.int32, rest[1].shape, 1)
        rest[1][...] = jnp.where(lane == 0, top, total)


def prefill(piece, pieces, q, bias, own, other, after, so_far):
    rows, width = q.shape
    blocks, _, half = own.shape
    steps, _, positions = bias.shape
    steps //= pieces
    whole = pl.BlockSpec((rows, KV_RANK), lambda i: (0, 0))
    stats = pl.BlockSpec((rows, 128), lambda i: (0, 0))
    last = piece == pieces - 1
    anywhere = pl.BlockSpec(memory_space=pl.ANY)
    buf = pltpu.VMEM((steps, blocks // pieces // steps, width, half), jnp.bfloat16)
    return pl.pallas_call(
        functools.partial(prefill_kernel, piece, pieces),
        grid=(1,),
        in_specs=[
            pl.BlockSpec((rows, width), lambda i: (0, 0)),
            pl.BlockSpec((steps, 1, positions), lambda i: (piece, 0, 0)),
            anywhere,
            anywhere,
            anywhere,
        ]
        + ([anywhere, stats] if so_far else []),
        out_specs=[whole, stats, pl.BlockSpec(memory_space=pltpu.VMEM)],
        out_shape=[
            jax.ShapeDtypeStruct((rows, KV_RANK), jnp.bfloat16 if last else jnp.float32),
            jax.ShapeDtypeStruct((rows, 128), jnp.float32),
            pltpu.VMEM((8, 128), jnp.float32),
        ],
        scratch_shapes=[
            buf,
            buf,
            pltpu.VMEM((rows, KV_RANK), jnp.float32),
            pltpu.SemaphoreType.DMA((2, steps)),
            pltpu.SemaphoreType.DMA,
        ],
        compiler_params=pltpu.CompilerParams(vmem_limit_bytes=BIG_VMEM),
        cost_estimate=pl.CostEstimate(
            flops=2 * rows * steps * positions * (width + KV_RANK),
            bytes_accessed=2 * steps * positions * width,
            transcendentals=rows * steps * positions,
        ),
        name="prefill",
    )(q, bias, own, other, after, *so_far[:2])


def expert_kernel(
    core_ref, x_ref, gain_ref, gate_hbm, up_hbm, down_hbm, keep_ref, send_ref, gate_buf, up_buf, down_buf, sems, down_sems
):
    halves, _, width = x_ref.shape
    parts, chunk, _ = gate_buf.shape
    core = core_ref[0]

    def copies(i):
        rows = pl.ds(i * chunk, chunk)
        return (
            pltpu.make_async_copy(gate_hbm.at[rows, :], gate_buf.at[i], sems.at[0, i]),
            pltpu.make_async_copy(up_hbm.at[rows, :], up_buf.at[i], sems.at[1, i]),
        )

    def down_copy(i):
        return pltpu.make_async_copy(
            down_hbm.at[:, pl.ds(i * chunk, chunk)], down_buf.at[i], down_sems.at[i]
        )

    def start(i):
        if i < parts:
            for copy in copies(i):
                copy.start()
        else:
            for j in range(2 * (i - parts), min(2 * (i - parts) + 2, parts)):
                down_copy(j).start()

    for i in range(AHEAD):
        start(i)
    square = 0.0
    for half in range(halves):
        x = x_ref[half].astype(jnp.float32)
        square = square + jnp.sum(x * x, axis=1, keepdims=True)
    scale = lax.rsqrt(square / (halves * width) + 1e-06)
    gate = up = None
    for i in range(parts):
        half, at = divmod(i * chunk, width)
        x = x_ref[half, :, at : at + chunk].astype(jnp.float32) * scale
        x = (x * gain_ref[:, i * chunk : (i + 1) * chunk]).astype(jnp.bfloat16)
        for copy in copies(i):
            copy.wait()
        start(i + AHEAD)
        g = jnp.dot(x, gate_buf[i], preferred_element_type=jnp.float32)
        u = jnp.dot(x, up_buf[i], preferred_element_type=jnp.float32)
        gate = g if gate is None else gate + g
        up = u if up is None else up + u
    inner = (jax.nn.silu(gate) * up).astype(jnp.bfloat16)
    for i in range(parts):
        down_copy(i).wait()
        if i % 2 == 1:
            start(parts + i // 2 + AHEAD)
        out = jnp.dot(inner, down_buf[i], preferred_element_type=jnp.float32).astype(jnp.bfloat16)
        half, at = divmod(i * chunk, width)

        @pl.when(core == half)
        def _():
            keep_ref[:, at : at + chunk] = out

        @pl.when(core != half)
        def _():
            send_ref[:, at : at + chunk] = out


def expert(core, x, gain, w_gate, w_up, w_down):
    _, rows, width = x.shape
    depth, hidden = w_gate.shape
    chunk = 896
    parts = depth // chunk
    vmem, anywhere = pl.BlockSpec(memory_space=pltpu.VMEM), pl.BlockSpec(memory_space=pl.ANY)
    return pl.pallas_call(
        expert_kernel,
        in_specs=[pl.BlockSpec(memory_space=pltpu.SMEM), vmem, vmem] + [anywhere] * 3,
        out_specs=[vmem, vmem],
        out_shape=[jax.ShapeDtypeStruct((rows, width), jnp.bfloat16)] * 2,
        scratch_shapes=[
            pltpu.VMEM((parts, chunk, hidden), jnp.bfloat16),
            pltpu.VMEM((parts, chunk, hidden), jnp.bfloat16),
            pltpu.VMEM((parts, hidden, chunk), jnp.bfloat16),
            pltpu.SemaphoreType.DMA((2, parts)),
            pltpu.SemaphoreType.DMA((parts,)),
        ],
        compiler_params=pltpu.CompilerParams(vmem_limit_bytes=EXPERT_VMEM),
        cost_estimate=pl.CostEstimate(
            flops=6 * rows * depth * hidden, bytes_accessed=6 * depth * hidden, transcendentals=rows * hidden
        ),
        name="expert",
    )(core, x, gain, w_gate, w_up, w_down)


def collect_kernel(extra, weight_ref, returned_ref, state_ref, dispatch_ref, *rest):
    added = jnp.dot(
        weight_ref[...],
        returned_ref[...].astype(jnp.float32),
        precision=lax.Precision.HIGHEST,
        preferred_element_type=jnp.float32,
    )
    state = (state_ref[...].astype(jnp.float32) + added).astype(jnp.bfloat16)
    outs = rest[extra:]
    outs[0][...] = state
    if len(outs) > 1:
        outs[1][...] = jnp.dot(dispatch_ref[...], state, preferred_element_type=jnp.float32).astype(jnp.bfloat16)


def collect_rows(weight, returned, state, dispatch, extra, last):
    vmem = pl.BlockSpec(memory_space=pltpu.VMEM)
    return pl.pallas_call(
        functools.partial(collect_kernel, len(extra)),
        in_specs=[vmem] * 4 + [pl.BlockSpec(memory_space=pl.ANY)] * len(extra),
        out_specs=[vmem] if last else [vmem, vmem],
        out_shape=[
            jax.ShapeDtypeStruct(state.shape, state.dtype),
            jax.ShapeDtypeStruct((dispatch.shape[0], state.shape[1]), state.dtype),
        ][: 1 if last else 2],
        compiler_params=pltpu.CompilerParams(vmem_limit_bytes=8 << 20),
        name="collect_rows",
    )(weight, returned, state, dispatch, *extra)


def per_device(
    stretch_queries,
    cache_latent,
    doc_lengths,
    decode_queries,
    w_attn_out,
    decode_hidden,
    norm_gain,
    w_gate,
    w_up,
    w_down,
    routes,
    gate_weights,
):
    tokens, heads, width = stretch_queries.shape
    rows, dec_heads, _ = decode_queries.shape
    block = cache_latent.shape[0]
    half = block // 2
    ctx_size = lax.axis_size(CTX)
    model = decode_hidden.shape[1]
    core = lax.axis_index("core")
    x_hi = lax.axis_index("x_hi")
    x_lo = lax.axis_index("x_lo")
    quarter = model // 4
    my_quarter = core * 2 + x_hi

    mine = lax.dynamic_slice_in_dim(cache_latent.T, core * half, half, 1)

    line = jnp.stack([mine] + [shift(mine, "y", by) for by in TURNS[1:]])
    dec_q = decode_queries.reshape(rows * dec_heads, width)
    group_q = spread(dec_q, SHARDS)
    shards = group_q.shape[0]
    plane = jnp.concatenate(
        [line]
        + [
            lax.ppermute(part, X, [(x_index(i), x_index(i + by)) for i in range(4)])
            for part, by in ((line[:2], 1), (line[2:], 3))
        ]
    )
    plane = tie(plane, group_q, vmem=12 << 20)
    plane_other = shift(plane, "core", 1)
    y = lax.axis_index("y")
    z = lax.axis_index("z")
    y_at = (y - jnp.array(TURNS, jnp.int32)) % 4

    def plane_at(z_at):
        return ((x_lo ^ jnp.arange(2, dtype=jnp.int32)[:, None]) * 4 + z_at) * 4 + y_at

    def lengths_of(blocks):
        hit = blocks[..., None] == jnp.arange(doc_lengths.shape[0], dtype=jnp.int32)
        return jnp.sum(jnp.where(hit, doc_lengths, 0), axis=-1)

    line_len = lengths_of(plane_at(z).reshape(8))
    place = jnp.arange(half, dtype=jnp.int32)

    def bias_of(which, lengths):
        usable = place + which * half < lengths[..., None]
        return jnp.where(usable, 0.0, MASKED).astype(jnp.float32)

    line_bias = jnp.stack([bias_of(core, line_len), bias_of(1 - core, line_len)])
    parts = decode_attention(
        group_q.reshape(shards * rows * dec_heads, width),
        (plane, plane_other),
        line_bias.reshape(1, 8 * block),
    )
    parts = lax.all_to_all(
        parts.reshape(shards, rows * dec_heads, KV_RANK + 128), SHARDS, 0, 0, tiled=True
    )
    dec_latent = pl.pallas_call(
        combine_kernel,
        out_shape=jax.ShapeDtypeStruct((rows * dec_heads, KV_RANK), jnp.bfloat16),
        compiler_params=pltpu.CompilerParams(vmem_limit_bytes=8 << 20),
        name="combine_shards",
    )(parts)

    all_latent = spread(dec_latent.reshape(rows, dec_heads * KV_RANK), CTX)
    cols = w_attn_out.shape[2]
    partial_attn = project(
        all_latent, jnp.swapaxes(w_attn_out, 1, 2)
    )
    both = lax.all_gather(partial_attn, "core", axis=0)
    attn_cols = jnp.sum(both.astype(jnp.float32), axis=0).astype(jnp.bfloat16)
    attn_cols = jnp.broadcast_to(
        attn_cols.reshape(ctx_size, 1, rows, cols), (ctx_size, 2, rows, cols)
    ).reshape(ctx_size * 2, rows, cols)
    attn_parts = lax.all_to_all(attn_cols, LANE, 0, 0, tiled=True)
    attn_parts = attn_parts.reshape(4, ctx_size // 4, 2, rows, cols)
    attn_parts = lax.dynamic_index_in_dim(attn_parts, my_quarter, 0, keepdims=False)
    attn_out = jnp.sum(attn_parts.astype(jnp.float32), axis=1).astype(jnp.bfloat16)
    attn_out = jnp.swapaxes(attn_out.reshape(8, rows, cols), 0, 1).reshape(rows, quarter)
    hidden_quarter = lax.dynamic_slice_in_dim(decode_hidden, my_quarter * quarter, quarter, 1)
    state = (hidden_quarter.astype(jnp.float32) + attn_out.astype(jnp.float32)).astype(jnp.bfloat16)

    experts = jnp.arange(ctx_size, dtype=jnp.int32)
    hits = routes[..., None] == experts
    used = jnp.any(hits, axis=2)
    weight = jnp.sum(jnp.where(hits, gate_weights[..., None], 0.0), axis=2)
    counted = used.astype(jnp.int32)
    earlier = jnp.cumsum(counted, axis=1) - counted
    placed = used[..., None] & (earlier[..., None] == jnp.arange(SLOTS, dtype=jnp.int32))
    dispatch = jnp.moveaxis(placed, 1, -1).astype(jnp.bfloat16)
    dispatch = jnp.broadcast_to(dispatch[:, :, None], (STEPS, ctx_size, 2, SLOTS, rows))
    dispatch = dispatch.reshape(STEPS, ctx_size * 2 * SLOTS, rows)
    collect = jnp.where(placed, weight[..., None], 0.0)
    collect = jnp.broadcast_to(collect[:, :, :, None, :], (STEPS, rows, ctx_size, 2, SLOTS))
    collect = collect.reshape(STEPS, rows, ctx_size * 2 * SLOTS)

    core_arr = core.astype(jnp.int32).reshape(1)
    gain = norm_gain.reshape(1, model)

    gathered = lax.all_gather(tie(plane, all_latent), "z", axis=0, tiled=True)
    all_len = lengths_of(plane_at(jnp.arange(4, dtype=jnp.int32)[:, None, None]).reshape(8, 4))
    bias = jnp.stack([bias_of(core, all_len), bias_of(1 - core, all_len)], axis=1)
    bias = bias.reshape(8, 1, KV_ARRAYS * 4 * half)
    flat_q = stretch_queries.reshape(tokens * heads, width)
    sums = ()

    outgoing = jnp.dot(dispatch[0], state, preferred_element_type=jnp.float32).astype(jnp.bfloat16)
    for step in range(STEPS):
        outgoing = outgoing.reshape(ctx_size * 2, SLOTS, quarter)
        received = lax.all_to_all(outgoing, LANE, 0, 0, tiled=True)
        if step > 0:
            sums = prefill(2 * step - 2, PIECES, flat_q, bias, *kv, outgoing, sums)
            received = tie(received, sums[2], vmem=4 << 20)
        received = received.reshape(ctx_size, 2, SLOTS, quarter)
        received = jnp.swapaxes(received, 1, 2).reshape(ctx_size * SLOTS, 2 * quarter)
        received = lax.all_gather(received, "core", axis=0)
        keep, send = expert(core_arr, received, gain, w_gate[0], w_up[0], w_down[0])
        partial_out = (keep.astype(jnp.float32) + shift(send, "core", 1).astype(jnp.float32)).astype(jnp.bfloat16)
        partial_out = partial_out.reshape(ctx_size, SLOTS, 2, quarter)
        partial_out = jnp.swapaxes(partial_out, 1, 2).reshape(ctx_size * 2, SLOTS, quarter)
        if step == 0:
            gathered = tie(gathered, partial_out)
            kv = [gathered, shift(gathered, "core", 1)]
        extra = []
        if step > 0:
            sums = prefill(2 * step - 1, PIECES, flat_q, bias, *kv, partial_out, sums)
            extra = [sums[2]]
        returned = lax.all_to_all(partial_out, LANE, 0, 0, tiled=True)
        returned = returned.reshape(ctx_size * 2 * SLOTS, quarter)
        last = step == STEPS - 1
        state, *outgoing = collect_rows(
            collect[step], returned, state, dispatch[min(step + 1, STEPS - 1)], extra, last
        )
        outgoing = None if last else outgoing[0]
    decode_out = lax.all_gather(state, HEAD, axis=0)
    decode_out = decode_out.reshape(2, 2, rows, quarter).transpose(2, 1, 0, 3).reshape(rows, model)
    return sums[0].reshape(tokens, heads, KV_RANK), decode_out


def solution(mesh):
    names = [name for axis in mesh.axis_names for name, _ in SPLIT[axis]]
    sizes = [size for axis in mesh.axis_names for _, size in SPLIT[axis]]
    fine = Mesh(mesh.devices.reshape(sizes), names)
    return jax.shard_map(
        per_device,
        mesh=fine,
        in_specs=(
            P(CTX, HEAD, None),
            P(CTX, None),
            P(),
            P(CTX, HEAD, None),
            P(HEAD, None, CTX),
            P(CTX, None),
            P(),
            P(CTX, None, HEAD),
            P(CTX, None, HEAD),
            P(CTX, HEAD, None),
            P(None, CTX, None),
            P(None, CTX, None),
        ),
        out_specs=(P(CTX, HEAD, None), P(CTX, None)),
        check_vma=False,
    )
```
